512 devices in a mesh: dp: 32 (over x, y_lo, core), vocab: 16 (over z, y_hi).
Axes of the slice: x: 4, y: 8 (y_hi: 2, y_lo: 4; y = y_hi * 4 + y_lo), z: 8, core: 2. Of those that a mesh axis runs over, the one named last changes fastest.
Arguments:
- hidden: bfloat16 [7168, 4096], P('dp'), may hold values from -6 to 6
- head_weight: bfloat16 [4096, 16384], P('dp', 'vocab'), may hold values from -0.09375 to 0.09375
- head_bias: float32 [16384], P('vocab'), may hold values from -1 to 1
- lengths: int32 [64, 2], P('dp'), may hold values from 1 to 80, as said below
- positives: int32 [64], P('dp'), may hold values from 0 to 63, each once
Outputs:
- hidden_grad: bfloat16 [7168, 4096], P(('dp', 'vocab'))
The draws below stay inside these ranges and needn't reach their ends.
Inputs may be any that keep to these rules, and one draw needn't show every extreme that they name: `lengths`: query counts are at most 32, passage counts at most 80; the first slots of each are used.
All inputs are finite; a program needn't handle non-finite values.
Results may differ from the reference program's by a relative error of at most 0.0064.
Values may be sent and summed in bfloat16 or wider, within the bound.
A program may use at most 64 MiB of HBM per device.

```python
import jax
import jax.numpy as jnp
from jax import lax

D = 4096
VS_DEV = 1024
QLEN = 32
PLEN = 80
PAIRS = 64
VOCAB = 16384
N_VOCAB = 16


def draw_hidden(key, part):
    key = jax.random.fold_in(key, 11)
    rows_pair = QLEN + PLEN
    values = jnp.clip(jax.random.normal(key, (PAIRS * rows_pair, D), jnp.float32), -4.0, 4.0)
    return values.astype(jnp.bfloat16)


def draw_lengths(key, part):
    key = jax.random.fold_in(key, 21)
    query_key = jax.random.fold_in(key, 22)
    passage_key = jax.random.fold_in(key, 23)
    order_key = jax.random.fold_in(key, 24)
    query_len = jax.random.randint(query_key, (PAIRS,), 1, QLEN + 1)
    passage_len = jax.random.randint(passage_key, (PAIRS,), 1, PLEN + 1)
    order = jax.random.permutation(order_key, PAIRS)
    query_len = query_len.at[order[0]].set(1).at[order[1]].set(QLEN)
    passage_len = passage_len.at[order[2]].set(PLEN)
    return jnp.stack([query_len, passage_len], axis=1).astype(jnp.int32)


def block_levels(stream_key, extent, split, low, largest):
    factor_of = 1.0
    for dim, parts in split:
        steps = jax.random.uniform(jax.random.fold_in(jax.random.fold_in(stream_key, 6), dim), (parts,), jnp.float32, low / len(split), largest / len(split))
        factor_of = factor_of * jnp.repeat(jnp.exp(steps), extent[dim] // parts).reshape((-1,) + (1,) * (len(extent) - 1 - dim))
    return factor_of


def noise(rng, shape, deviation, bound, cuts=(), kind=jnp.bfloat16):
    values = deviation * jax.random.normal(rng, shape, jnp.float32)
    if cuts:
        values = values * block_levels(rng, shape, cuts, -0.22, 0.18)
    return jnp.clip(values, -bound, bound).astype(kind)


def setup_inputs(seed: int = 0) -> dict:
    keys = jax.random.split(jax.random.key(seed), 6)
    return {
        "hidden": draw_hidden(jax.random.fold_in(keys[5], 71), 0),
        "head_weight": noise(keys[1], (D, VOCAB), D ** -0.5, 0.09375, ((0, 32), (1, 16))),
        "head_bias": jnp.clip(jax.random.uniform(keys[2], (VOCAB,), jnp.float32, -1.0, 1.0) * block_levels(keys[2], (VOCAB,), ((0, 16),), -0.4, 0.0), -1.0, 1.0),
        "lengths": draw_lengths(jax.random.fold_in(keys[5], 71), 0),
        "positives": jax.random.permutation(keys[4], PAIRS).astype(jnp.int32),
    }


POOL_TEMP = 0.25
SCORE_TEMP = 0.01
LOSS_SCALE = 65536.0


def row_mask(lengths, rows_pair):
    position = lax.broadcasted_iota(jnp.int32, (1, rows_pair), 1)
    is_query = position < QLEN
    offset = jnp.where(is_query, position, position - QLEN)
    limit_len = jnp.where(is_query, lengths[:, 0:1], lengths[:, 1:2])
    return (offset < limit_len).astype(jnp.float32)


def pool_terms(logits, token_mask):
    softened = jax.nn.softplus(logits)
    boosted = token_mask[:, :, None] * jnp.exp(jnp.log1p(softened) / POOL_TEMP)
    return softened, boosted


def pooled_vectors(boosted, lengths):
    query_sum = jnp.sum(boosted[:, :QLEN], axis=1)
    passage_sum = jnp.sum(boosted[:, QLEN:], axis=1)
    query_vec = POOL_TEMP * jnp.log(query_sum / lengths[:, 0:1].astype(jnp.float32))
    passage_vec = POOL_TEMP * jnp.log(passage_sum / lengths[:, 1:2].astype(jnp.float32))
    return query_vec, passage_vec, query_sum, passage_sum


def score_grads(scores, positives, pair_count):
    row_max = jnp.max(scores, axis=1, keepdims=True)
    shifted = jnp.exp(scores - row_max)
    softmax_out = shifted / jnp.sum(shifted, axis=1, keepdims=True)
    target = (positives[:, None] == lax.broadcasted_iota(jnp.int32, (1, pair_count), 1)).astype(jnp.float32)
    return LOSS_SCALE * (softmax_out - target)


def logit_grads(logits, softened, boosted, query_sum, passage_sum, query_grad, passage_grad):
    pairs_here = logits.shape[0]
    rest_rows = logits.shape[1] - QLEN
    entries = logits.shape[2]
    query_side = jnp.broadcast_to((query_grad / query_sum)[:, None, :], (pairs_here, QLEN, entries))
    passage_side = jnp.broadcast_to((passage_grad / passage_sum)[:, None, :], (pairs_here, rest_rows, entries))
    per_token = jnp.concatenate([query_side, passage_side], axis=1)
    slope = jax.nn.sigmoid(logits) / (1.0 + softened)
    return (boosted * slope * per_token).astype(jnp.bfloat16)


def reference(hidden, head_weight, head_bias, lengths, positives):
    rows_pair = QLEN + PLEN
    token_mask = row_mask(lengths, rows_pair)
    head_blocks = jnp.transpose(head_weight.reshape(D, N_VOCAB, VS_DEV), (1, 0, 2))
    bias_blocks = head_bias.reshape(N_VOCAB, VS_DEV)

    def block_logits(block_weight, block_bias):
        flat_logits = jnp.dot(hidden, block_weight, preferred_element_type=jnp.float32) + block_bias
        return flat_logits.reshape(PAIRS, rows_pair, VS_DEV)

    def pool_block(operands):
        logits = block_logits(operands[0], operands[1])
        pooled = pooled_vectors(pool_terms(logits, token_mask)[1], lengths)
        return pooled[0], pooled[1]

    query_blocks, passage_blocks = lax.map(pool_block, (head_blocks, bias_blocks))
    query_vec = jnp.transpose(query_blocks, (1, 0, 2)).reshape(PAIRS, VOCAB).astype(jnp.bfloat16)
    passage_vec = jnp.transpose(passage_blocks, (1, 0, 2)).reshape(PAIRS, VOCAB).astype(jnp.bfloat16)
    score_scale = 1.0 / (SCORE_TEMP * VOCAB)
    scores = score_scale * lax.dot_general(query_vec, passage_vec, (((1,), (1,)), ((), ())), preferred_element_type=jnp.float32)
    score_grad = score_grads(scores, positives, PAIRS)
    query_grad = score_scale * jnp.dot(score_grad, passage_vec.astype(jnp.float32), precision=lax.Precision.HIGHEST)
    passage_grad = score_scale * lax.dot_general(score_grad, query_vec.astype(jnp.float32), (((0,), (0,)), ((), ())), precision=lax.Precision.HIGHEST)
    query_grad_blocks = jnp.transpose(query_grad.reshape(PAIRS, N_VOCAB, VS_DEV), (1, 0, 2))
    passage_grad_blocks = jnp.transpose(passage_grad.reshape(PAIRS, N_VOCAB, VS_DEV), (1, 0, 2))

    def add_block(running, operands):
        block_weight, block_bias, query_part, passage_part = operands
        logits = block_logits(block_weight, block_bias)
        softened, boosted = pool_terms(logits, token_mask)
        pooled = pooled_vectors(boosted, lengths)
        logit_grad = logit_grads(logits, softened, boosted, pooled[2], pooled[3], query_part, passage_part)
        logit_grad = logit_grad.reshape(PAIRS * rows_pair, VS_DEV)
        update = lax.dot_general(logit_grad, block_weight, (((1,), (1,)), ((), ())), preferred_element_type=jnp.float32)
        return running + update, None

    initial = jnp.zeros((PAIRS * rows_pair, D), jnp.float32)
    summed, unused = lax.scan(add_block, initial, (head_blocks, bias_blocks, query_grad_blocks, passage_grad_blocks))
    return summed.astype(jnp.bfloat16)
```

```python
import jax
import jax.numpy as jnp
from jax import lax
from jax.experimental import pallas as pl
from jax.experimental.pallas import tpu as pltpu
from jax.sharding import PartitionSpec as P

QLEN = 32
PLEN = 80
ROWS_PAIR = QLEN + PLEN
ROWS = 2 * ROWS_PAIR
WIDTH = 4096
SLICE = 1024
SHARD = 128
HALF = 64
PAIRS = 64

POOL_TEMP = 0.25
SCORE_TEMP = 0.01
LOSS_SCALE = 65536.0
SCORE_SCALE = 1.0 / (SCORE_TEMP * 16384)

GROUP = 16
OWN = 14
CHUNK = 2 * GROUP
STREAMS = 8
COLS = WIDTH // STREAMS

BF = jnp.bfloat16
F32 = jnp.float32
MESH = pl.DeviceIdType.MESH

SEGMENTS = (
    (0, QLEN),
    (ROWS_PAIR, QLEN),
    (QLEN, PLEN),
    (ROWS_PAIR + QLEN, PLEN),
)


def kernel(
    hidden_ref, weight_ref, bias_ref, lengths_ref, positives_ref, out_ref,
    hid, wf, act, sums, vecs, packed, pooled, select, spread, both, part_scores, score_parts,
    grads, grads_t, targets, lgrad, part, chain_out, chain_in, kept, swap_out, swap_in,
    local_sem, w_send, w_recv, t_send, t_recv, v_send, v_recv, g_send, g_recv,
    s_send, s_recv, d_send, d_recv, c_send, c_recv, y_send, y_recv,
):
    dp = lax.axis_index("dp")
    vocab = lax.axis_index("vocab")
    x, y, core = dp // 8, (dp // 2) % 4, dp % 2
    z, hi = vocab // 2, vocab % 2
    xc = x * 2 + core

    def dp_of(xx, yy, cc):
        return (xx * 4 + yy) * 2 + cc

    load_w = pltpu.make_async_copy(weight_ref, wf.at[pl.ds(pl.multiple_of(dp * SHARD, SHARD), SHARD)], local_sem.at[0])
    load_h = pltpu.make_async_copy(hidden_ref, hid, local_sem.at[1])
    load_w.start()
    load_h.start()

    y_peers = [dp_of(x, (y + o) % 4, core) for o in range(1, 4)]
    xc_peers = [(xc + o) % 8 for o in range(1, 8)]
    xc_dp = [dp_of(p // 2, y, p % 2) for p in xc_peers]
    vocab_peers = [(vocab + o) % 16 for o in range(1, 16)]

    barrier = pltpu.get_barrier_semaphore()
    for p in y_peers + xc_dp:
        pl.semaphore_signal(barrier, inc=1, device_id={"dp": p, "vocab": vocab}, device_id_type=MESH)
    for p in vocab_peers:
        pl.semaphore_signal(barrier, inc=1, device_id={"dp": dp, "vocab": p}, device_id_type=MESH)

    row = lax.broadcasted_iota(jnp.int32, (128, 512), 0)
    col = lax.broadcasted_iota(jnp.int32, (128, 512), 1)
    pair = row % PAIRS
    first = (pair // 2) * 16 + pair % 2 + jnp.where(row < PAIRS, 2, 0)
    for i in range(4):
        select[i] = jnp.where(col == first + 4 * i, 1.0, 0.0).astype(BF)
    prow = lax.broadcasted_iota(jnp.int32, (256, 256), 0)
    pcol = lax.broadcasted_iota(jnp.int32, (256, 256), 1)
    wanted = (prow // GROUP) * OWN + prow % GROUP
    spread[...] = jnp.where((pcol == wanted) & (prow % GROUP < OWN), 1.0, 0.0).astype(BF)
    lgrad[pl.ds(ROWS, 32), :] = jnp.zeros((32, SLICE), BF)
    act[...] = jnp.broadcast_to(bias_ref[...], (ROWS, SLICE))

    trow = lax.broadcasted_iota(jnp.int32, (8, 128), 0)
    tcol = lax.broadcasted_iota(jnp.int32, (8, 128), 1)
    tile = jnp.zeros((8, 128), F32)
    for j in range(2):
        k = positives_ref[j]
        place = (k // 16) * 16 + ((k // 2) % 2) * 8 + ((k // 4) % 4) * 2 + k % 2
        tile = tile + jnp.where((trow == 2 * y + j) & (tcol == place), 1.0, 0.0)
    targets[y] = tile

    load_w.wait()
    pl.semaphore_wait(barrier, 25)

    sends = []

    def remote(src, dst, send_sem, recv_sem, to_dp, to_vocab):
        copy = pltpu.make_async_remote_copy(
            src_ref=src, dst_ref=dst, send_sem=send_sem, recv_sem=recv_sem,
            device_id={"dp": to_dp, "vocab": to_vocab}, device_id_type=MESH,
        )
        copy.start()
        return copy

    def unit(slot, h):
        return wf.at[pl.ds(pl.multiple_of(slot * SHARD + h * HALF, HALF), HALF)]

    def arrived(slot, h):
        pltpu.make_async_copy(unit(slot, h), unit(slot, h), w_recv.at[slot * 2 + h]).wait()

    count = [0]

    def send(slot, h, to, cond=None):
        n = count[0]
        count[0] += 1
        copy = pltpu.make_async_remote_copy(
            src_ref=unit(slot, h), dst_ref=unit(slot, h), send_sem=w_send.at[n], recv_sem=w_recv.at[slot * 2 + h],
            device_id={"dp": to, "vocab": vocab}, device_id_type=MESH,
        )
        if cond is None:
            copy.start()
        else:
            pl.when(cond)(copy.start)
        sends.append((cond, copy))

    right, left, far = (x + 1) % 4, (x + 3) % 4, (x + 2) % 4
    sibling = dp_of(x, y, 1 - core)

    def line_place(t):
        low = jnp.where(y < 2, y, 3 - y)
        place = jnp.where((low == 1) & (t < 2), 1 - t, t)
        return jnp.where(y < 2, place, 3 - place)

    def own_column(t):
        yy = line_place(t)
        slot = dp_of(x, yy, core)
        for h in range(2):
            if t == 0:
                send(slot, h, dp_of(x, jnp.minimum(y + 1, 3), core), y < 3)
                send(slot, h, dp_of(x, jnp.maximum(y - 1, 0), core), y > 0)
            else:
                arrived(slot, h)
                send(slot, h, dp_of(x, jnp.minimum(y + 1, 3), core), (yy < y) & (y < 3))
                send(slot, h, dp_of(x, jnp.maximum(y - 1, 0), core), (yy > y) & (y > 0))
            send(slot, h, dp_of(right, y, core))
            send(slot, h, dp_of(left, y, core))
            send(slot, h, sibling)

    def neighbours(t):
        yy = line_place(t)
        for h in range(2):
            slot = dp_of(left, yy, core)
            arrived(slot, h)
            if h == 0:
                send(slot, h, dp_of(right, y, core))
            send(slot, h, sibling)
            slot = dp_of(right, yy, core)
            arrived(slot, h)
            if h == 1:
                send(slot, h, dp_of(left, y, core))
            send(slot, h, sibling)

    def last(t):
        yy = line_place(t)
        slot = dp_of(far, yy, core)
        for h in range(2):
            arrived(slot, h)
            send(slot, h, sibling)

    def dots(t):
        yy = line_place(t)

        def step(i, carry):
            chip = ((x + i) % 4) * 4 + yy
            for h in range(2):
                arrived(chip * 2 + 1 - core, h)
            deep = pl.ds(pl.multiple_of(chip * 256, 256), 256)
            act[...] += jnp.dot(hid[:, deep], wf[deep, :], preferred_element_type=F32)
            return carry

        lax.fori_loop(0, 4, step, 0)

    own_column(0)
    t_copies = [
        remote(targets.at[y], targets.at[y], t_send.at[i], t_recv.at[y], p, vocab) for i, p in enumerate(y_peers)
    ]
    load_h.wait()
    own_column(1)
    neighbours(0)
    own_column(2)
    neighbours(1)
    last(0)
    dots(0)
    own_column(3)
    neighbours(2)
    last(1)
    dots(1)
    neighbours(3)
    last(2)
    dots(2)
    last(3)
    dots(3)

    def pool(b, carry):
        cols = pl.ds(pl.multiple_of(b * 128, 128), 128)
        for n, (start, size) in enumerate(SEGMENTS):
            length = lengths_ref[n % 2, n // 2]
            logits = act[pl.ds(start, size), cols]
            position = lax.broadcasted_iota(jnp.int32, (size, 128), 0)
            mask = jnp.where(position < length, 1.0, 0.0).astype(F32)
            small = jnp.exp(-jnp.abs(logits))
            above = 1.0 + jnp.maximum(logits, 0.0) + jnp.log1p(small)
            slope = jnp.where(logits >= 0.0, 1.0, small) / (1.0 + small)
            cubed = mask * (above * above * above)
            total = jnp.sum(cubed * above, axis=0, keepdims=True)
            act[pl.ds(start, size), cols] = cubed * slope
            sums[pl.ds(n, 1), cols] = total
            vecs[pl.ds(n, 1), cols] = POOL_TEMP * jnp.log(total / length.astype(F32))
        return carry

    lax.fori_loop(0, 8, pool, 0)
    for i in range(4):
        packed[pl.ds(4 * i, 4), :] = vecs[pl.ds(0, 4), pl.ds(256 * i, 256)]
    mine = xc * 4 + y
    pooled[mine] = packed[...].astype(BF)

    v_copies = [
        remote(pooled.at[mine], pooled.at[mine], v_send.at[i], v_recv.at[y], p, vocab) for i, p in enumerate(y_peers)
    ]
    for o in range(1, 4):
        yy = (y + o) % 4
        pltpu.make_async_copy(pooled.at[xc * 4 + yy], pooled.at[xc * 4 + yy], v_recv.at[yy]).wait()
    line = pl.ds(xc * 4, 4)
    g_copies = [
        remote(pooled.at[line], pooled.at[line], g_send.at[i], g_recv.at[xc], p, vocab) for i, p in enumerate(xc_dp)
    ]
    for p in xc_peers:
        block = pooled.at[pl.ds(p * 4, 4)]
        pltpu.make_async_copy(block, block, g_recv.at[p]).wait()

    flat = pooled[...].reshape(512, 256)
    for i in range(4):
        both[:, pl.ds(256 * i, 256)] = jnp.dot(select[i], flat, preferred_element_type=F32).astype(BF)
    nt = (((1,), (1,)), ((), ()))
    part_scores[...] = lax.dot_general(both[pl.ds(PAIRS, PAIRS), :], both[...], nt, preferred_element_type=F32)

    rows8 = pl.ds(pl.multiple_of(xc * 8, 8), 8)
    score_parts[vocab] = part_scores[rows8, :]
    s_copies = [
        remote(score_parts.at[vocab], score_parts.at[vocab], s_send.at[i], s_recv.at[vocab], dp, p)
        for i, p in enumerate(vocab_peers)
    ]
    for o in range(1, 4):
        yy = (y + o) % 4
        pltpu.make_async_copy(targets.at[yy], targets.at[yy], t_recv.at[yy]).wait()
    target = targets[0] + targets[1] + targets[2] + targets[3]
    for p in vocab_peers:
        pltpu.make_async_copy(score_parts.at[p], score_parts.at[p], s_recv.at[p]).wait()
    scores = SCORE_SCALE * jnp.sum(score_parts[...], axis=0)
    valid = tcol < PAIRS
    top = jnp.max(jnp.where(valid, scores, -jnp.inf), axis=1, keepdims=True)
    shifted = jnp.where(valid, jnp.exp(jnp.where(valid, scores - top, 0.0)), 0.0)
    soft = shifted / jnp.sum(shifted, axis=1, keepdims=True)
    grads[pl.ds(xc, 1)] = (LOSS_SCALE * (soft - target)).reshape(1, 8, 128)
    d_copies = [
        remote(grads.at[xc], grads.at[xc], d_send.at[i], d_recv.at[xc], p, vocab) for i, p in enumerate(xc_dp)
    ]
    for p in xc_peers:
        pltpu.make_async_copy(grads.at[p], grads.at[p], d_recv.at[p]).wait()
    whole = jnp.concatenate([grads[...].reshape(PAIRS, 128), jnp.zeros((PAIRS, 128), F32)], axis=0)
    grads_t[...] = whole.T

    def exact_dot(lhs, rhs):
        a = lhs.astype(BF)
        rest = lhs - a.astype(F32)
        b = rest.astype(BF)
        c = (rest - b.astype(F32)).astype(BF)
        out = jnp.dot(c, rhs, preferred_element_type=F32)
        out = out + jnp.dot(b, rhs, preferred_element_type=F32)
        return out + jnp.dot(a, rhs, preferred_element_type=F32)

    q_grad = exact_dot(grads[pl.ds(xc, 1)].reshape(8, 128)[:, :PAIRS], both[pl.ds(0, PAIRS), :])
    p_grad = exact_dot(grads_t[rows8, :][:, :PAIRS], both[pl.ds(PAIRS, PAIRS), :])
    srow = lax.broadcasted_iota(jnp.int32, (8, SLICE), 0)
    for n, (start, size) in enumerate(SEGMENTS):
        grad = q_grad if n < 2 else p_grad
        one = jnp.sum(jnp.where(srow == 2 * y + n % 2, grad, 0.0), axis=0, keepdims=True)
        vecs[pl.ds(n, 1), :] = (SCORE_SCALE * one) / sums[pl.ds(n, 1), :]

    def finish(b, carry):
        cols = pl.ds(pl.multiple_of(b * 128, 128), 128)
        for n, (start, size) in enumerate(SEGMENTS):
            lgrad[pl.ds(start, size), cols] = (act[pl.ds(start, size), cols] * vecs[pl.ds(n, 1), cols]).astype(BF)
        return carry

    lax.fori_loop(0, 8, finish, 0)
    lgrad[...] = jnp.dot(spread[...], lgrad[...], preferred_element_type=F32).astype(BF)

    up, down = ((z + 1) % 8) * 2 + hi, ((z + 7) % 8) * 2 + hi
    across = z * 2 + 1 - hi
    c_copies = []

    def place(k):
        return pl.ds(pl.multiple_of(((z + k + 8) % 8) * CHUNK, CHUNK), CHUNK)

    def hop(c, i, value, to):
        chain_out[c, i] = value.astype(BF)
        c_copies.append(remote(chain_out.at[c, i], chain_in.at[c, i], c_send.at[c, i], c_recv.at[c, i], dp, to))

    def landed(c, i):
        pltpu.make_async_copy(chain_in.at[c, i], chain_in.at[c, i], c_recv.at[c, i]).wait()
        return chain_in[c, i].astype(F32)

    def advance(c, s):
        a = 4 if c % 2 == 0 else 3
        b = 7 - a
        cols = pl.ds(c * COLS, COLS)
        if s == 0:
            part[:, cols] = lax.dot_general(lgrad[...], wf[cols, :], nt, preferred_element_type=F32)
            hop(c, 0, part[place(a), cols], up)
            hop(c, a, part[place(-b), cols], down)
        elif s < 4:
            if s < a:
                hop(c, s, landed(c, s - 1) + part[place(a - s), cols], up)
            if s < b:
                hop(c, a + s, landed(c, a + s - 1) + part[place(s - b), cols], down)
        elif s == 4:
            total = part[place(0), cols] + landed(c, a - 1) + landed(c, 6)
            kept[c] = total
            swap_out[c] = kept[c, pl.ds(pl.multiple_of((1 - hi) * GROUP, GROUP), GROUP), :].astype(BF)
            c_copies.append(remote(swap_out.at[c], swap_in.at[c], y_send.at[c], y_recv.at[c], dp, across))
        else:
            pltpu.make_async_copy(swap_in.at[c], swap_in.at[c], y_recv.at[c]).wait()
            total = kept[c, pl.ds(pl.multiple_of(hi * GROUP, GROUP), GROUP), :] + swap_in[c].astype(F32)
            out_ref[:, cols] = total[:OWN].astype(BF)

    for t in range(STREAMS + 5):
        for c in range(STREAMS):
            if 0 <= t - c <= 5:
                advance(c, t - c)

    for cond, copy in sends:
        if cond is None:
            copy.wait_send()
        else:
            pl.when(cond)(copy.wait_send)
    for copy in t_copies + v_copies + g_copies + s_copies + d_copies + c_copies:
        copy.wait_send()


def per_device(hidden, head_weight, head_bias, lengths, positives):
    vmem, smem = pltpu.VMEM, pltpu.SMEM
    dma = pltpu.SemaphoreType.DMA
    return pl.pallas_call(
        kernel,
        out_shape=jax.ShapeDtypeStruct((OWN, WIDTH), BF),
        in_specs=[
            pl.BlockSpec(memory_space=pl.ANY),
            pl.BlockSpec(memory_space=pl.ANY),
            pl.BlockSpec(memory_space=vmem),
            pl.BlockSpec(memory_space=smem),
            pl.BlockSpec(memory_space=smem),
        ],
        out_specs=pl.BlockSpec(memory_space=vmem),
        scratch_shapes=[
            vmem((ROWS, WIDTH), BF),
            vmem((WIDTH, SLICE), BF),
            vmem((ROWS, SLICE), F32),
            vmem((8, SLICE), F32),
            vmem((8, SLICE), F32),
            vmem((16, 256), F32),
            vmem((32, 16, 256), BF),
            vmem((4, 128, 512), BF),
            vmem((256, 256), BF),
            vmem((128, SLICE), BF),
            vmem((PAIRS, 128), F32),
            vmem((16, 8, 128), F32),
            vmem((8, 8, 128), F32),
            vmem((128, 128), F32),
            vmem((4, 8, 128), F32),
            vmem((256, SLICE), BF),
            vmem((256, WIDTH), F32),
            vmem((STREAMS, 7, CHUNK, COLS), BF),
            vmem((STREAMS, 7, CHUNK, COLS), BF),
            vmem((STREAMS, CHUNK, COLS), F32),
            vmem((STREAMS, GROUP, COLS), BF),
            vmem((STREAMS, GROUP, COLS), BF),
            dma((2,)),
            dma((96,)), dma((64,)),
            dma((3,)), dma((4,)),
            dma((3,)), dma((4,)),
            dma((7,)), dma((8,)),
            dma((15,)), dma((16,)),
            dma((7,)), dma((8,)),
            dma((STREAMS, 7)), dma((STREAMS, 7)),
            dma((STREAMS,)), dma((STREAMS,)),
        ],
        compiler_params=pltpu.CompilerParams(
            collective_id=0, has_side_effects=True, vmem_limit_bytes=48 * 1024 * 1024
        ),
        cost_estimate=pl.CostEstimate(flops=4 * ROWS * WIDTH * SLICE, bytes_accessed=4 * 1024 * 1024, transcendentals=3 * ROWS * SLICE),
    )(hidden, head_weight, head_bias.reshape(1, SLICE), lengths, positives)


def solution(mesh):
    return jax.shard_map(
        per_device,
        mesh=mesh,
        in_specs=(P("dp", None), P("dp", "vocab"), P("vocab"), P("dp", None), P("dp")),
        out_specs=P(("dp", "vocab"), None),
        check_vma=False,
    )
```

```python
import jax
import jax.numpy as jnp
from jax import lax
from jax.experimental import pallas as pl
from jax.experimental.pallas import tpu as pltpu
from jax.sharding import PartitionSpec as P

QLEN = 32
PLEN = 80
ROWS_PAIR = QLEN + PLEN
ROWS = 2 * ROWS_PAIR
WIDTH = 4096
SLICE = 1024
SHARD = 128
PAIRS = 64

POOL_TEMP = 0.25
SCORE_TEMP = 0.01
LOSS_SCALE = 65536.0
SCORE_SCALE = 1.0 / (SCORE_TEMP * 16384)

GROUP = 16
OWN = 14
CHUNK = 2 * GROUP
STREAMS = 8
COLS = WIDTH // STREAMS
EARLY = 1
LAG = 8

BF = jnp.bfloat16
F32 = jnp.float32
MESH = pl.DeviceIdType.MESH

SEGMENTS = (
    (0, QLEN),
    (ROWS_PAIR, QLEN),
    (QLEN, PLEN),
    (ROWS_PAIR + QLEN, PLEN),
)


def kernel(
    hidden_ref, weight_ref, bias_hbm, lengths_hbm, positives_hbm, out_ref,
    bias_ref, lengths_ref, positives_ref, hid, wf, act, sums, vecs, packed, pooled, select, spread, both, part_scores, score_parts,
    grads, grads_t, targets, lgrad, part, chain_out, chain_in, kept, swap_out, swap_in,
    wide_out, wide_in, near_out, near_in, summed,
    local_sem, w_send, w_recv, t_send, t_recv, v_send, v_recv, g_send, g_recv,
    s_send, s_recv, d_send, d_recv, c_send, c_recv, y_send, y_recv,
):
    dp = lax.axis_index("dp")
    vocab = lax.axis_index("vocab")
    x, y, core = dp // 8, (dp // 2) % 4, dp % 2
    z, hi = vocab // 2, vocab % 2
    xc = x * 2 + core

    def dp_of(xx, yy, cc):
        return (xx * 4 + yy) * 2 + cc

    load_w = pltpu.make_async_copy(weight_ref, wf.at[pl.ds(pl.multiple_of(dp * SHARD, SHARD), SHARD)], local_sem.at[0])
    load_h = pltpu.make_async_copy(hidden_ref, hid, local_sem.at[1])
    loads = [
        load_w,
        load_h,
        pltpu.make_async_copy(bias_hbm, bias_ref, local_sem.at[2]),
        pltpu.make_async_copy(lengths_hbm, lengths_ref, local_sem.at[3]),
        pltpu.make_async_copy(positives_hbm, positives_ref, local_sem.at[4]),
    ]
    for load in loads:
        load.start()

    y_peers = [dp_of(x, (y + o) % 4, core) for o in range(1, 4)]
    xc_peers = [(xc + o) % 8 for o in range(1, 8)]
    xc_dp = [dp_of(p // 2, y, p % 2) for p in xc_peers]
    vocab_peers = [(vocab + o) % 16 for o in range(1, 16)]

    barrier = pltpu.get_barrier_semaphore()
    for p in y_peers + xc_dp:
        pl.semaphore_signal(barrier, inc=1, device_id={"dp": p, "vocab": vocab}, device_id_type=MESH)
    for p in vocab_peers:
        pl.semaphore_signal(barrier, inc=1, device_id={"dp": dp, "vocab": p}, device_id_type=MESH)

    load_w.wait()
    pl.semaphore_wait(barrier, 25)

    sends = []
    copies = []

    def remote(src, dst, send_sem, recv_sem, to_dp, to_vocab):
        copy = pltpu.make_async_remote_copy(
            src_ref=src, dst_ref=dst, send_sem=send_sem, recv_sem=recv_sem,
            device_id={"dp": to_dp, "vocab": to_vocab}, device_id_type=MESH,
        )
        copy.start()
        copies.append(copy)

    UNITS = ((0, 64), (64, 48), (112, 16))
    FIRST, REST = (0, 1), 2

    def unit(slot, u):
        start, size = UNITS[u]
        return wf.at[pl.ds(pl.multiple_of(slot * SHARD + start, 16), size)]

    def w_sem(slot, u):
        return w_recv.at[slot * 3 + u]

    def arrived(slot, u):
        pltpu.make_async_copy(unit(slot, u), unit(slot, u), w_sem(slot, u)).wait()

    count = [0]

    def send(slot, u, to, cond=None):
        n = count[0]
        count[0] += 1
        copy = pltpu.make_async_remote_copy(
            src_ref=unit(slot, u), dst_ref=unit(slot, u), send_sem=w_send.at[n], recv_sem=w_sem(slot, u),
            device_id={"dp": to, "vocab": vocab}, device_id_type=MESH,
        )
        if cond is None:
            copy.start()
        else:
            pl.when(cond)(copy.start)
        sends.append((cond, copy))

    right, left, far = (x + 1) % 4, (x + 3) % 4, (x + 2) % 4
    to_right, to_left = dp_of(right, y, core), dp_of(left, y, core)
    above, below = dp_of(x, jnp.minimum(y + 1, 3), core), dp_of(x, jnp.maximum(y - 1, 0), core)
    sibling = dp_of(x, y, 1 - core)

    def line_place(t):
        low = jnp.where(y < 2, y, 3 - y)
        place = jnp.where((low == 1) & (t < 2), 1 - t, t)
        return jnp.where(y < 2, place, 3 - place)

    def onward(slot, u, yy):
        rising = yy < y
        send(slot, u, jnp.where(rising, above, below), (rising & (y < 3)) | ((yy > y) & (y > 0)))

    def both_ways(slot, u):
        send(slot, u, above, y < 3)
        send(slot, u, below, y > 0)

    def column(t):
        yy = line_place(t)
        slot = dp_of(x, yy, core)
        for u in FIRST:
            if t == 0:
                both_ways(slot, u)
            else:
                arrived(slot, u)
                onward(slot, u, yy)
            send(slot, u, to_right)
            send(slot, u, to_left)
            send(slot, u, sibling)

    def relay(u, yy):
        rightward = (yy + u) % 2 == 0
        slot = dp_of(jnp.where(rightward, left, right), yy, core)
        arrived(slot, u)
        send(slot, u, jnp.where(rightward, to_right, to_left))
        send(slot, u, sibling)
        slot = dp_of(jnp.where(rightward, right, left), yy, core)
        arrived(slot, u)
        send(slot, u, sibling)

    def neighbours(t):
        for u in FIRST:
            relay(u, line_place(t))

    def last(t):
        slot = dp_of(far, line_place(t), core)
        for u in FIRST:
            arrived(slot, u)
            send(slot, u, sibling)

    def rest_own():
        send(dp, REST, to_right)
        send(dp, REST, to_left)
        send(dp, REST, sibling)

    def rest_neighbours():
        relay(REST, y)

    def rest_out():
        for source in (x, left, right):
            both_ways(dp_of(source, y, core), REST)

    def rest_last():
        slot = dp_of(far, y, core)
        arrived(slot, REST)
        both_ways(slot, REST)
        send(slot, REST, sibling)

    def rest_line(t):
        yy = line_place(t)
        for source in (x, left, right, far):
            slot = dp_of(source, yy, core)
            arrived(slot, REST)
            onward(slot, REST, yy)
            send(slot, REST, sibling)

    def dots(t):
        yy = line_place(t)

        def step(i, carry):
            chip = ((x + 3 + i) % 4) * 4 + yy
            for u in FIRST + (REST,):
                arrived(chip * 2 + 1 - core, u)
            deep = pl.ds(pl.multiple_of(chip * 256, 256), 256)
            act[...] += jnp.dot(hid[:, deep], wf[deep, :], preferred_element_type=F32)
            return carry

        lax.fori_loop(0, 4, step, 0)

    column(0)
    rest_own()

    for load in loads[1:]:
        load.wait()

    row = lax.broadcasted_iota(jnp.int32, (128, 512), 0)
    col = lax.broadcasted_iota(jnp.int32, (128, 512), 1)
    pair = row % PAIRS
    first = (pair // 2) * 16 + pair % 2 + jnp.where(row < PAIRS, 2, 0)
    for i in range(4):
        select[i] = jnp.where(col == first + 4 * i, 1.0, 0.0).astype(BF)
    prow = lax.broadcasted_iota(jnp.int32, (256, 256), 0)
    pcol = lax.broadcasted_iota(jnp.int32, (256, 256), 1)
    wanted = (prow // GROUP) * OWN + prow % GROUP
    spread[...] = jnp.where((pcol == wanted) & (prow % GROUP < OWN), 1.0, 0.0).astype(BF)
    lgrad[pl.ds(ROWS, 32), :] = jnp.zeros((32, SLICE), BF)
    act[...] = jnp.broadcast_to(bias_ref[...], (ROWS, SLICE))

    trow = lax.broadcasted_iota(jnp.int32, (8, 128), 0)
    tcol = lax.broadcasted_iota(jnp.int32, (8, 128), 1)
    tile = jnp.zeros((8, 128), F32)
    for j in range(2):
        k = positives_ref[j]
        place = (k // 16) * 16 + ((k // 2) % 2) * 8 + ((k // 4) % 4) * 2 + k % 2
        tile = tile + jnp.where((trow == 2 * y + j) & (tcol == place), 1.0, 0.0)
    targets[y] = tile

    for i, p in enumerate(y_peers):
        remote(targets.at[y], targets.at[y], t_send.at[i], t_recv.at[y], p, vocab)
    column(1)
    neighbours(0)
    column(2)
    rest_neighbours()
    neighbours(1)
    column(3)
    rest_out()
    last(0)
    rest_last()
    neighbours(2)
    rest_line(1)
    last(1)
    neighbours(3)
    rest_line(2)
    last(2)
    rest_line(3)
    last(3)
    for t in range(4):
        dots(t)
    for o in range(1, 4):
        yy = (y + o) % 4
        pltpu.make_async_copy(targets.at[yy], targets.at[yy], t_recv.at[yy]).wait()

    def pool(b, carry):
        cols = pl.ds(pl.multiple_of(b * 128, 128), 128)
        for n, (start, size) in enumerate(SEGMENTS):
            length = lengths_ref[n % 2, n // 2]
            logits = act[pl.ds(start, size), cols]
            position = lax.broadcasted_iota(jnp.int32, (size, 128), 0)
            mask = jnp.where(position < length, 1.0, 0.0).astype(F32)
            small = jnp.exp(-jnp.abs(logits))
            above = 1.0 + jnp.maximum(logits, 0.0) + jnp.log1p(small)
            slope = jnp.where(logits >= 0.0, 1.0, small) / (1.0 + small)
            cubed = mask * (above * above * above)
            total = jnp.sum(cubed * above, axis=0, keepdims=True)
            act[pl.ds(start, size), cols] = cubed * slope
            sums[pl.ds(n, 1), cols] = total
            vecs[pl.ds(n, 1), cols] = POOL_TEMP * jnp.log(total / length.astype(F32))
        return carry

    lax.fori_loop(0, 8, pool, 0)
    for i in range(4):
        packed[pl.ds(4 * i, 4), :] = vecs[pl.ds(0, 4), pl.ds(256 * i, 256)]
    mine = xc * 4 + y
    pooled[mine] = packed[...].astype(BF)

    for i, p in enumerate(y_peers):
        remote(pooled.at[mine], pooled.at[mine], v_send.at[i], v_recv.at[y], p, vocab)
    for o in range(1, 4):
        yy = (y + o) % 4
        pltpu.make_async_copy(pooled.at[xc * 4 + yy], pooled.at[xc * 4 + yy], v_recv.at[yy]).wait()
    line = pl.ds(xc * 4, 4)
    for i, p in enumerate(xc_dp):
        remote(pooled.at[line], pooled.at[line], g_send.at[i], g_recv.at[xc], p, vocab)
    for p in xc_peers:
        block = pooled.at[pl.ds(p * 4, 4)]
        pltpu.make_async_copy(block, block, g_recv.at[p]).wait()

    flat = pooled[...].reshape(512, 256)
    for i in range(4):
        both[:, pl.ds(256 * i, 256)] = jnp.dot(select[i], flat, preferred_element_type=F32).astype(BF)
    nt = (((1,), (1,)), ((), ()))
    part_scores[...] = lax.dot_general(both[pl.ds(PAIRS, PAIRS), :], both[...], nt, preferred_element_type=F32)

    rows8 = pl.ds(pl.multiple_of(xc * 8, 8), 8)
    score_parts[vocab] = part_scores[rows8, :]
    for i, p in enumerate(vocab_peers):
        remote(score_parts.at[vocab], score_parts.at[vocab], s_send.at[i], s_recv.at[vocab], dp, p)
    target = targets[0] + targets[1] + targets[2] + targets[3]
    for p in vocab_peers:
        pltpu.make_async_copy(score_parts.at[p], score_parts.at[p], s_recv.at[p]).wait()
    scores = SCORE_SCALE * jnp.sum(score_parts[...], axis=0)
    valid = tcol < PAIRS
    top = jnp.max(jnp.where(valid, scores, -jnp.inf), axis=1, keepdims=True)
    shifted = jnp.where(valid, jnp.exp(jnp.where(valid, scores - top, 0.0)), 0.0)
    soft = shifted / jnp.sum(shifted, axis=1, keepdims=True)
    grads[pl.ds(xc, 1)] = (LOSS_SCALE * (soft - target)).reshape(1, 8, 128)
    for i, p in enumerate(xc_dp):
        remote(grads.at[xc], grads.at[xc], d_send.at[i], d_recv.at[xc], p, vocab)
    for p in xc_peers:
        pltpu.make_async_copy(grads.at[p], grads.at[p], d_recv.at[p]).wait()
    whole = jnp.concatenate([grads[...].reshape(PAIRS, 128), jnp.zeros((PAIRS, 128), F32)], axis=0)
    grads_t[...] = whole.T

    def exact_dot(lhs, rhs):
        a = lhs.astype(BF)
        rest = lhs - a.astype(F32)
        b = rest.astype(BF)
        c = (rest - b.astype(F32)).astype(BF)
        out = jnp.dot(c, rhs, preferred_element_type=F32)
        out = out + jnp.dot(b, rhs, preferred_element_type=F32)
        return out + jnp.dot(a, rhs, preferred_element_type=F32)

    q_grad = exact_dot(grads[pl.ds(xc, 1)].reshape(8, 128)[:, :PAIRS], both[pl.ds(0, PAIRS), :])
    p_grad = exact_dot(grads_t[rows8, :][:, :PAIRS], both[pl.ds(PAIRS, PAIRS), :])
    srow = lax.broadcasted_iota(jnp.int32, (8, SLICE), 0)
    for n, (start, size) in enumerate(SEGMENTS):
        grad = q_grad if n < 2 else p_grad
        one = jnp.sum(jnp.where(srow == 2 * y + n % 2, grad, 0.0), axis=0, keepdims=True)
        vecs[pl.ds(n, 1), :] = (SCORE_SCALE * one) / sums[pl.ds(n, 1), :]

    def finish(b, carry):
        cols = pl.ds(pl.multiple_of(b * 128, 128), 128)
        for n, (start, size) in enumerate(SEGMENTS):
            lgrad[pl.ds(start, size), cols] = (act[pl.ds(start, size), cols] * vecs[pl.ds(n, 1), cols]).astype(BF)
        return carry

    lax.fori_loop(0, 8, finish, 0)
    lgrad[...] = jnp.dot(spread[...], lgrad[...], preferred_element_type=F32).astype(BF)

    up, down = ((z + 1) % 8) * 2 + hi, ((z + 7) % 8) * 2 + hi
    across = z * 2 + 1 - hi

    def cols_of(c):
        return pl.ds(c * COLS, COLS)

    def own_part(c, k):
        place = (z + k + 8) % 8
        if c < EARLY:
            return summed[c, place]
        return part[pl.ds(pl.multiple_of(place * CHUNK, CHUNK), CHUNK), cols_of(c)]

    def hop(c, i, value, to):
        if c < EARLY:
            out_slot, in_slot = near_out.at[c, i], near_in.at[c, i]
        else:
            out_slot, in_slot = chain_out.at[c - EARLY, i], chain_in.at[c - EARLY, i]
        out_slot[...] = value.astype(BF)
        remote(out_slot, in_slot, c_send.at[c, i], c_recv.at[c, i], dp, to)

    def landed(c, i):
        in_slot = near_in.at[c, i] if c < EARLY else chain_in.at[c - EARLY, i]
        pltpu.make_async_copy(in_slot, in_slot, c_recv.at[c, i]).wait()
        return in_slot[...].astype(F32)

    def chain(c, s):
        a = 4 if c % 2 == 0 else 3
        b = 7 - a
        if s == 0:
            hop(c, 0, own_part(c, a), up)
            hop(c, a, own_part(c, -b), down)
        elif s < 4:
            if s < a:
                hop(c, s, landed(c, s - 1) + own_part(c, a - s), up)
            if s < b:
                hop(c, a + s, landed(c, a + s - 1) + own_part(c, s - b), down)
        else:
            return own_part(c, 0) + landed(c, a - 1) + landed(c, 6)

    def product(c):
        part[:, cols_of(c)] = lax.dot_general(lgrad[...], wf[cols_of(c), :], nt, preferred_element_type=F32)

    def group(c, place, h):
        return part[pl.ds(pl.multiple_of(place * CHUNK + h * GROUP, GROUP), GROUP), cols_of(c)]

    def early(c, s):
        if s == 0:
            product(c)
            for place in range(8):
                wide_out[c, place] = group(c, place, 1 - hi).astype(BF)
            remote(wide_out.at[c], wide_in.at[c], y_send.at[c], y_recv.at[c], dp, across)
        elif s == 1:
            pltpu.make_async_copy(wide_in.at[c], wide_in.at[c], y_recv.at[c]).wait()
            for place in range(8):
                summed[c, place] = group(c, place, hi) + wide_in[c, place].astype(F32)
            chain(c, 0)
        elif s < 5:
            chain(c, s - 1)
        else:
            out_ref[:, cols_of(c)] = chain(c, 4)[:OWN].astype(BF)

    def late(c, s):
        if s == 0:
            product(c)
        if s < 4:
            chain(c, s)
        elif s == 4:
            kept[c] = chain(c, 4)
            swap_out[c] = kept[c, pl.ds(pl.multiple_of((1 - hi) * GROUP, GROUP), GROUP), :].astype(BF)
            remote(swap_out.at[c], swap_in.at[c], y_send.at[c], y_recv.at[c], dp, across)
        else:
            pltpu.make_async_copy(swap_in.at[c], swap_in.at[c], y_recv.at[c]).wait()
            total = kept[c, pl.ds(pl.multiple_of(hi * GROUP, GROUP), GROUP), :] + swap_in[c].astype(F32)
            out_ref[:, cols_of(c)] = total[:OWN].astype(BF)

    def when(c, s):
        if c < EARLY:
            return (STREAMS * s + c + (LAG if s else 0), c)
        return (STREAMS * s + c, c)

    for c, s in sorted(((c, s) for c in range(STREAMS) for s in range(6)), key=lambda e: when(*e)):
        (early if c < EARLY else late)(c, s)

    for cond, copy in sends:
        if cond is None:
            copy.wait_send()
        else:
            pl.when(cond)(copy.wait_send)
    for copy in copies:
        copy.wait_send()


def per_device(hidden, head_weight, head_bias, lengths, positives):
    vmem, smem = pltpu.VMEM, pltpu.SMEM
    dma = pltpu.SemaphoreType.DMA
    return pl.pallas_call(
        kernel,
        out_shape=jax.ShapeDtypeStruct((OWN, WIDTH), BF),
        in_specs=[
            pl.BlockSpec(memory_space=pl.ANY),
            pl.BlockSpec(memory_space=pl.ANY),
            pl.BlockSpec(memory_space=pl.ANY),
            pl.BlockSpec(memory_space=pl.ANY),
            pl.BlockSpec(memory_space=pl.ANY),
        ],
        out_specs=pl.BlockSpec(memory_space=vmem),
        scratch_shapes=[
            vmem((1, SLICE), F32),
            smem((2, 2), jnp.int32),
            smem((2,), jnp.int32),
            vmem((ROWS, WIDTH), BF),
            vmem((WIDTH, SLICE), BF),
            vmem((ROWS, SLICE), F32),
            vmem((8, SLICE), F32),
            vmem((8, SLICE), F32),
            vmem((16, 256), F32),
            vmem((32, 16, 256), BF),
            vmem((4, 128, 512), BF),
            vmem((256, 256), BF),
            vmem((128, SLICE), BF),
            vmem((PAIRS, 128), F32),
            vmem((16, 8, 128), F32),
            vmem((8, 8, 128), F32),
            vmem((128, 128), F32),
            vmem((4, 8, 128), F32),
            vmem((256, SLICE), BF),
            vmem((256, WIDTH), F32),
            vmem((STREAMS - EARLY, 7, CHUNK, COLS), BF),
            vmem((STREAMS - EARLY, 7, CHUNK, COLS), BF),
            vmem((STREAMS, CHUNK, COLS), F32),
            vmem((STREAMS, GROUP, COLS), BF),
            vmem((STREAMS, GROUP, COLS), BF),
            vmem((EARLY, 8, GROUP, COLS), BF),
            vmem((EARLY, 8, GROUP, COLS), BF),
            vmem((EARLY, 7, GROUP, COLS), BF),
            vmem((EARLY, 7, GROUP, COLS), BF),
            vmem((EARLY, 8, GROUP, COLS), F32),
            dma((5,)),
            dma((128,)), dma((96,)),
            dma((3,)), dma((4,)),
            dma((3,)), dma((4,)),
            dma((7,)), dma((8,)),
            dma((15,)), dma((16,)),
            dma((7,)), dma((8,)),
            dma((STREAMS, 7)), dma((STREAMS, 7)),
            dma((STREAMS,)), dma((STREAMS,)),
        ],
        compiler_params=pltpu.CompilerParams(
            collective_id=0, has_side_effects=True, vmem_limit_bytes=63 * 1024 * 1024
        ),
        cost_estimate=pl.CostEstimate(flops=4 * ROWS * WIDTH * SLICE, bytes_accessed=4 * 1024 * 1024, transcendentals=3 * ROWS * SLICE),
    )(hidden, head_weight, head_bias.reshape(1, SLICE), lengths, positives)


def solution(mesh):
    return jax.shard_map(
        per_device,
        mesh=mesh,
        in_specs=(P("dp", None), P("dp", "vocab"), P("vocab"), P("dp", None), P("dp")),
        out_specs=P(("dp", "vocab"), None),
        check_vma=False,
    )
```

```python
import jax
import jax.numpy as jnp
from jax import lax
from jax.experimental import pallas as pl
from jax.experimental.pallas import tpu as pltpu
from jax.sharding import PartitionSpec as P

QLEN = 32
PLEN = 80
ROWS_PAIR = QLEN + PLEN
ROWS = 2 * ROWS_PAIR
WIDTH = 4096
SLICE = 1024
SHARD = 128
PAIRS = 64

POOL_TEMP = 0.25
SCORE_TEMP = 0.01
LOSS_SCALE = 65536.0
SCORE_SCALE = 1.0 / (SCORE_TEMP * 16384)

GROUP = 16
OWN = 14
CHUNK = 2 * GROUP
STREAMS = 8
COLS = WIDTH // STREAMS
EARLY = 1
LAG = 8

BF = jnp.bfloat16
F32 = jnp.float32
MESH = pl.DeviceIdType.MESH

SEGMENTS = (
    (0, QLEN),
    (ROWS_PAIR, QLEN),
    (QLEN, PLEN),
    (ROWS_PAIR + QLEN, PLEN),
)


def kernel(
    hidden_ref, weight_ref, bias_hbm, lengths_hbm, positives_hbm, out_ref,
    bias_ref, lengths_ref, positives_ref, hid, wf, act, sums, vecs, packed, pooled, select, spread, both, twice, part_scores, score_parts,
    grads, grads_t, targets, row_targets, lgrad, part, chain_out, chain_in, kept, swap_out, swap_in,
    wide_out, wide_in, near_out, near_in, summed,
    local_sem, w_send, w_recv, t_send, t_recv, u_send, u_recv, v_send, v_recv, g_send, g_recv,
    s_send, s_recv, d_send, d_recv, c_send, c_recv, y_send, y_recv,
):
    dp = lax.axis_index("dp")
    vocab = lax.axis_index("vocab")
    x, y, core = dp // 8, (dp // 2) % 4, dp % 2
    z, hi = vocab // 2, vocab % 2
    xc = core * 4 + x

    def dp_of(xx, yy, cc):
        return (xx * 4 + yy) * 2 + cc

    load_w = pltpu.make_async_copy(weight_ref, wf.at[pl.ds(pl.multiple_of(dp * SHARD, SHARD), SHARD)], local_sem.at[0])
    load_h = pltpu.make_async_copy(hidden_ref, hid, local_sem.at[1])
    loads = [
        load_w,
        load_h,
        pltpu.make_async_copy(bias_hbm, bias_ref, local_sem.at[2]),
        pltpu.make_async_copy(lengths_hbm, lengths_ref, local_sem.at[3]),
        pltpu.make_async_copy(positives_hbm, positives_ref, local_sem.at[4]),
    ]
    for load in loads:
        load.start()

    y_peers = [dp_of(x, (y + o) % 4, core) for o in range(1, 4)]
    xc_peers = [(xc + o) % 8 for o in range(1, 8)]
    xc_dp = [dp_of(p % 4, y, p // 4) for p in xc_peers]
    vocab_peers = [(vocab + o) % 16 for o in range(1, 16)]

    barrier = pltpu.get_barrier_semaphore()
    for p in y_peers + xc_dp:
        pl.semaphore_signal(barrier, inc=1, device_id={"dp": p, "vocab": vocab}, device_id_type=MESH)
    for p in vocab_peers:
        pl.semaphore_signal(barrier, inc=1, device_id={"dp": dp, "vocab": p}, device_id_type=MESH)

    load_w.wait()
    pl.semaphore_wait(barrier, 25)

    sends = []
    copies = []

    def remote(src, dst, send_sem, recv_sem, to_dp, to_vocab):
        copy = pltpu.make_async_remote_copy(
            src_ref=src, dst_ref=dst, send_sem=send_sem, recv_sem=recv_sem,
            device_id={"dp": to_dp, "vocab": to_vocab}, device_id_type=MESH,
        )
        copy.start()
        copies.append(copy)

    UNITS = ((0, 64), (64, 48), (112, 16))
    FIRST, REST = (0, 1), 2

    def unit(slot, u):
        start, size = UNITS[u]
        return wf.at[pl.ds(pl.multiple_of(slot * SHARD + start, 16), size)]

    def w_sem(slot, u):
        return w_recv.at[slot * 3 + u]

    def arrived(slot, u):
        pltpu.make_async_copy(unit(slot, u), unit(slot, u), w_sem(slot, u)).wait()

    count = [0]

    def send(slot, u, to, cond=None):
        n = count[0]
        count[0] += 1
        copy = pltpu.make_async_remote_copy(
            src_ref=unit(slot, u), dst_ref=unit(slot, u), send_sem=w_send.at[n], recv_sem=w_sem(slot, u),
            device_id={"dp": to, "vocab": vocab}, device_id_type=MESH,
        )
        if cond is None:
            copy.start()
        else:
            pl.when(cond)(copy.start)
        sends.append((cond, copy))

    right, left, far = (x + 1) % 4, (x + 3) % 4, (x + 2) % 4
    to_right, to_left = dp_of(right, y, core), dp_of(left, y, core)
    above, below = dp_of(x, jnp.minimum(y + 1, 3), core), dp_of(x, jnp.maximum(y - 1, 0), core)
    sibling = dp_of(x, y, 1 - core)

    def line_place(t):
        low = jnp.where(y < 2, y, 3 - y)
        place = jnp.where((low == 1) & (t < 2), 1 - t, t)
        return jnp.where(y < 2, place, 3 - place)

    def onward(slot, u, yy):
        rising = yy < y
        send(slot, u, jnp.where(rising, above, below), (rising & (y < 3)) | ((yy > y) & (y > 0)))

    def both_ways(slot, u):
        send(slot, u, above, y < 3)
        send(slot, u, below, y > 0)

    def column(t):
        yy = line_place(t)
        slot = dp_of(x, yy, core)
        for u in FIRST:
            if t == 0:
                both_ways(slot, u)
            else:
                arrived(slot, u)
                onward(slot, u, yy)
            send(slot, u, to_right)
            send(slot, u, to_left)
            send(slot, u, sibling)

    def relay(u, yy):
        rightward = (yy + u) % 2 == 0
        slot = dp_of(jnp.where(rightward, left, right), yy, core)
        arrived(slot, u)
        send(slot, u, jnp.where(rightward, to_right, to_left))
        send(slot, u, sibling)
        slot = dp_of(jnp.where(rightward, right, left), yy, core)
        arrived(slot, u)
        send(slot, u, sibling)

    def neighbours(t):
        for u in FIRST:
            relay(u, line_place(t))

    def last(t):
        slot = dp_of(far, line_place(t), core)
        for u in FIRST:
            arrived(slot, u)
            send(slot, u, sibling)

    def rest_own():
        send(dp, REST, to_right)
        send(dp, REST, to_left)
        send(dp, REST, sibling)

    def rest_neighbours():
        relay(REST, y)

    def rest_out():
        for source in (x, left, right):
            both_ways(dp_of(source, y, core), REST)

    def rest_last():
        slot = dp_of(far, y, core)
        arrived(slot, REST)
        both_ways(slot, REST)
        send(slot, REST, sibling)

    def rest_line(t):
        yy = line_place(t)
        for source in (x, left, right, far):
            slot = dp_of(source, yy, core)
            arrived(slot, REST)
            onward(slot, REST, yy)
            send(slot, REST, sibling)

    def dots(t):
        yy = line_place(t)

        def step(i, carry):
            chip = ((x + 3 + i) % 4) * 4 + yy
            for u in FIRST + (REST,):
                arrived(chip * 2 + 1 - core, u)
            deep = pl.ds(pl.multiple_of(chip * 256, 256), 256)
            act[...] += jnp.dot(hid[:, deep], wf[deep, :], preferred_element_type=F32)
            return carry

        lax.fori_loop(0, 4, step, 0)

    column(0)
    rest_own()

    for load in loads[1:]:
        load.wait()

    row = lax.broadcasted_iota(jnp.int32, (128, 512), 0)
    col = lax.broadcasted_iota(jnp.int32, (128, 512), 1)
    pair = row % PAIRS
    first = (pair // 2) * 16 + pair % 2 + jnp.where(row < PAIRS, 2, 0)
    for i in range(4):
        select[i] = jnp.where(col == first + 4 * i, 1.0, 0.0).astype(BF)
    prow = lax.broadcasted_iota(jnp.int32, (256, 256), 0)
    pcol = lax.broadcasted_iota(jnp.int32, (256, 256), 1)
    wanted = (prow // GROUP) * OWN + prow % GROUP
    spread[...] = jnp.where((pcol == wanted) & (prow % GROUP < OWN), 1.0, 0.0).astype(BF)
    lgrad[pl.ds(ROWS, 32), :] = jnp.zeros((32, SLICE), BF)
    act[...] = jnp.broadcast_to(bias_ref[...], (ROWS, SLICE))

    trow = lax.broadcasted_iota(jnp.int32, (8, 128), 0)
    tcol = lax.broadcasted_iota(jnp.int32, (8, 128), 1)
    tile = jnp.zeros((8, 128), F32)
    for j in range(2):
        k = positives_ref[j]
        place = ((k // 2) % 2) * 32 + (k // 16) * 8 + ((k // 4) % 4) * 2 + k % 2
        tile = tile + jnp.where((trow == 2 * y + j) & (tcol == place), 1.0, 0.0)
    targets[y] = tile

    for i, p in enumerate(y_peers):
        remote(targets.at[y], targets.at[y], t_send.at[i], t_recv.at[y], p, vocab)
    column(1)
    neighbours(0)
    column(2)
    rest_neighbours()
    neighbours(1)
    column(3)
    rest_out()
    for o in range(1, 4):
        yy = (y + o) % 4
        pltpu.make_async_copy(targets.at[yy], targets.at[yy], t_recv.at[yy]).wait()
    row_targets[x] = targets[0] + targets[1] + targets[2] + targets[3]
    for i, p in enumerate((right, left, far)):
        remote(row_targets.at[x], row_targets.at[x], u_send.at[i], u_recv.at[x], dp_of(p, y, core), vocab)
    last(0)
    rest_last()
    neighbours(2)
    rest_line(1)
    last(1)
    neighbours(3)
    rest_line(2)
    last(2)
    rest_line(3)
    last(3)
    for t in range(4):
        dots(t)
    for o in range(1, 4):
        block = row_targets.at[(x + o) % 4]
        pltpu.make_async_copy(block, block, u_recv.at[(x + o) % 4]).wait()

    def pool(b, carry):
        cols = pl.ds(pl.multiple_of(b * 128, 128), 128)
        for n, (start, size) in enumerate(SEGMENTS):
            length = lengths_ref[n % 2, n // 2]
            logits = act[pl.ds(start, size), cols]
            position = lax.broadcasted_iota(jnp.int32, (size, 128), 0)
            mask = jnp.where(position < length, 1.0, 0.0).astype(F32)
            small = jnp.exp(-jnp.abs(logits))
            above = 1.0 + jnp.maximum(logits, 0.0) + jnp.log1p(small)
            slope = jnp.where(logits >= 0.0, 1.0, small) / (1.0 + small)
            cubed = mask * (above * above * above)
            total = jnp.sum(cubed * above, axis=0, keepdims=True)
            act[pl.ds(start, size), cols] = cubed * slope
            sums[pl.ds(n, 1), cols] = total
            vecs[pl.ds(n, 1), cols] = POOL_TEMP * jnp.log(total / length.astype(F32))
        return carry

    lax.fori_loop(0, 8, pool, 0)
    for i in range(4):
        packed[pl.ds(4 * i, 4), :] = vecs[pl.ds(0, 4), pl.ds(256 * i, 256)]
    mine = xc * 4 + y
    pooled[mine] = packed[...].astype(BF)

    for i, p in enumerate(y_peers):
        remote(pooled.at[mine], pooled.at[mine], v_send.at[i], v_recv.at[y], p, vocab)
    for o in range(1, 4):
        yy = (y + o) % 4
        pltpu.make_async_copy(pooled.at[xc * 4 + yy], pooled.at[xc * 4 + yy], v_recv.at[yy]).wait()
    line = pl.ds(xc * 4, 4)
    for i, p in enumerate(xc_dp):
        remote(pooled.at[line], pooled.at[line], g_send.at[i], g_recv.at[xc], p, vocab)
    for p in xc_peers:
        block = pooled.at[pl.ds(p * 4, 4)]
        pltpu.make_async_copy(block, block, g_recv.at[p]).wait()

    flat = pooled[...].reshape(512, 256)
    for i in range(4):
        both[:, pl.ds(256 * i, 256)] = jnp.dot(select[i], flat, preferred_element_type=F32).astype(BF)
    passages = both[pl.ds(0, PAIRS), :]
    twice[pl.ds(0, PAIRS), :] = passages
    twice[pl.ds(PAIRS, PAIRS), :] = passages
    nt = (((1,), (1,)), ((), ()))
    part_scores[...] = lax.dot_general(both[pl.ds(PAIRS, PAIRS), :], twice[...], nt, preferred_element_type=F32)

    rows8 = pl.ds(pl.multiple_of(xc * 8, 8), 8)
    low_lanes = lax.broadcasted_iota(jnp.int32, (16, 128), 1) < PAIRS
    first_rows = pl.ds(pl.multiple_of(core * 32, 16), 16)
    next_rows = pl.ds(pl.multiple_of(core * 32 + 16, 16), 16)
    score_parts[vocab] = jnp.where(low_lanes, part_scores[first_rows, :], part_scores[next_rows, :])
    for i, p in enumerate(vocab_peers):
        remote(score_parts.at[vocab], score_parts.at[vocab], s_send.at[i], s_recv.at[vocab], dp, p)
    for p in vocab_peers:
        pltpu.make_async_copy(score_parts.at[p], score_parts.at[p], s_recv.at[p]).wait()
    summed_parts = jnp.sum(score_parts[...], axis=0)
    scores = SCORE_SCALE * jnp.concatenate([summed_parts, pltpu.roll(summed_parts, PAIRS, 1)], axis=0)
    valid = lax.broadcasted_iota(jnp.int32, (32, 128), 1) < PAIRS
    top = jnp.max(jnp.where(valid, scores, -jnp.inf), axis=1, keepdims=True)
    shifted = jnp.where(valid, jnp.exp(jnp.where(valid, scores - top, 0.0)), 0.0)
    soft = shifted / jnp.sum(shifted, axis=1, keepdims=True)
    grads[pl.ds(core, 1)] = (LOSS_SCALE * (soft - row_targets[...].reshape(32, 128))).reshape(1, 32, 128)
    remote(grads.at[core], grads.at[core], d_send.at[0], d_recv.at[core], sibling, vocab)
    pltpu.make_async_copy(grads.at[1 - core], grads.at[1 - core], d_recv.at[1 - core]).wait()
    whole = jnp.concatenate([grads[...].reshape(PAIRS, 128), jnp.zeros((PAIRS, 128), F32)], axis=0)
    grads_t[...] = whole.T

    def exact_dot(lhs, rhs):
        a = lhs.astype(BF)
        rest = lhs - a.astype(F32)
        b = rest.astype(BF)
        c = (rest - b.astype(F32)).astype(BF)
        out = jnp.dot(c, rhs, preferred_element_type=F32)
        out = out + jnp.dot(b, rhs, preferred_element_type=F32)
        return out + jnp.dot(a, rhs, preferred_element_type=F32)

    rows8_here = pl.ds(pl.multiple_of(x * 8, 8), 8)
    q_grad = exact_dot(grads[core, rows8_here, :][:, :PAIRS], both[pl.ds(0, PAIRS), :])
    p_grad = exact_dot(grads_t[rows8, :][:, :PAIRS], both[pl.ds(PAIRS, PAIRS), :])
    srow = lax.broadcasted_iota(jnp.int32, (8, SLICE), 0)
    for n, (start, size) in enumerate(SEGMENTS):
        grad = q_grad if n < 2 else p_grad
        one = jnp.sum(jnp.where(srow == 2 * y + n % 2, grad, 0.0), axis=0, keepdims=True)
        vecs[pl.ds(n, 1), :] = (SCORE_SCALE * one) / sums[pl.ds(n, 1), :]

    def finish(b, carry):
        cols = pl.ds(pl.multiple_of(b * 128, 128), 128)
        for n, (start, size) in enumerate(SEGMENTS):
            lgrad[pl.ds(start, size), cols] = (act[pl.ds(start, size), cols] * vecs[pl.ds(n, 1), cols]).astype(BF)
        return carry

    lax.fori_loop(0, 8, finish, 0)
    lgrad[...] = jnp.dot(spread[...], lgrad[...], preferred_element_type=F32).astype(BF)

    up, down = ((z + 1) % 8) * 2 + hi, ((z + 7) % 8) * 2 + hi
    across = z * 2 + 1 - hi

    def cols_of(c):
        return pl.ds(c * COLS, COLS)

    def own_part(c, k):
        place = (z + k + 8) % 8
        if c < EARLY:
            return summed[c, place]
        return part[pl.ds(pl.multiple_of(place * CHUNK, CHUNK), CHUNK), cols_of(c)]

    def hop(c, i, value, to):
        if c < EARLY:
            out_slot, in_slot = near_out.at[c, i], near_in.at[c, i]
        else:
            out_slot, in_slot = chain_out.at[c - EARLY, i], chain_in.at[c - EARLY, i]
        out_slot[...] = value.astype(BF)
        remote(out_slot, in_slot, c_send.at[c, i], c_recv.at[c, i], dp, to)

    def landed(c, i):
        in_slot = near_in.at[c, i] if c < EARLY else chain_in.at[c - EARLY, i]
        pltpu.make_async_copy(in_slot, in_slot, c_recv.at[c, i]).wait()
        return in_slot[...].astype(F32)

    def chain(c, s):
        a = 4 if c % 2 == 0 else 3
        b = 7 - a
        if s == 0:
            hop(c, 0, own_part(c, a), up)
            hop(c, a, own_part(c, -b), down)
        elif s < 4:
            if s < a:
                hop(c, s, landed(c, s - 1) + own_part(c, a - s), up)
            if s < b:
                hop(c, a + s, landed(c, a + s - 1) + own_part(c, s - b), down)
        else:
            return own_part(c, 0) + landed(c, a - 1) + landed(c, 6)

    def product(c):
        part[:, cols_of(c)] = lax.dot_general(lgrad[...], wf[cols_of(c), :], nt, preferred_element_type=F32)

    def group(c, place, h):
        return part[pl.ds(pl.multiple_of(place * CHUNK + h * GROUP, GROUP), GROUP), cols_of(c)]

    def early(c, s):
        if s == 0:
            product(c)
            for place in range(8):
                wide_out[c, place] = group(c, place, 1 - hi).astype(BF)
            remote(wide_out.at[c], wide_in.at[c], y_send.at[c], y_recv.at[c], dp, across)
        elif s == 1:
            pltpu.make_async_copy(wide_in.at[c], wide_in.at[c], y_recv.at[c]).wait()
            for place in range(8):
                summed[c, place] = group(c, place, hi) + wide_in[c, place].astype(F32)
            chain(c, 0)
        elif s < 5:
            chain(c, s - 1)
        else:
            out_ref[:, cols_of(c)] = chain(c, 4)[:OWN].astype(BF)

    def late(c, s):
        if s == 0:
            product(c)
        if s < 4:
            chain(c, s)
        elif s == 4:
            kept[c] = chain(c, 4)
            swap_out[c] = kept[c, pl.ds(pl.multiple_of((1 - hi) * GROUP, GROUP), GROUP), :].astype(BF)
            remote(swap_out.at[c], swap_in.at[c], y_send.at[c], y_recv.at[c], dp, across)
        else:
            pltpu.make_async_copy(swap_in.at[c], swap_in.at[c], y_recv.at[c]).wait()
            total = kept[c, pl.ds(pl.multiple_of(hi * GROUP, GROUP), GROUP), :] + swap_in[c].astype(F32)
            out_ref[:, cols_of(c)] = total[:OWN].astype(BF)

    def when(c, s):
        if c < EARLY:
            return (STREAMS * s + c + (LAG if s else 0), c)
        return (STREAMS * s + c, c)

    for c, s in sorted(((c, s) for c in range(STREAMS) for s in range(6)), key=lambda e: when(*e)):
        (early if c < EARLY else late)(c, s)

    for cond, copy in sends:
        if cond is None:
            copy.wait_send()
        else:
            pl.when(cond)(copy.wait_send)
    for copy in copies:
        copy.wait_send()


def per_device(hidden, head_weight, head_bias, lengths, positives):
    vmem, smem = pltpu.VMEM, pltpu.SMEM
    dma = pltpu.SemaphoreType.DMA
    return pl.pallas_call(
        kernel,
        out_shape=jax.ShapeDtypeStruct((OWN, WIDTH), BF),
        in_specs=[
            pl.BlockSpec(memory_space=pl.ANY),
            pl.BlockSpec(memory_space=pl.ANY),
            pl.BlockSpec(memory_space=pl.ANY),
            pl.BlockSpec(memory_space=pl.ANY),
            pl.BlockSpec(memory_space=pl.ANY),
        ],
        out_specs=pl.BlockSpec(memory_space=vmem),
        scratch_shapes=[
            vmem((1, SLICE), F32),
            smem((2, 2), jnp.int32),
            smem((2,), jnp.int32),
            vmem((ROWS, WIDTH), BF),
            vmem((WIDTH, SLICE), BF),
            vmem((ROWS, SLICE), F32),
            vmem((8, SLICE), F32),
            vmem((8, SLICE), F32),
            vmem((16, 256), F32),
            vmem((32, 16, 256), BF),
            vmem((4, 128, 512), BF),
            vmem((256, 256), BF),
            vmem((128, SLICE), BF),
            vmem((128, SLICE), BF),
            vmem((PAIRS, 128), F32),
            vmem((16, 16, 128), F32),
            vmem((2, 32, 128), F32),
            vmem((128, 128), F32),
            vmem((4, 8, 128), F32),
            vmem((4, 8, 128), F32),
            vmem((256, SLICE), BF),
            vmem((256, WIDTH), F32),
            vmem((STREAMS - EARLY, 7, CHUNK, COLS), BF),
            vmem((STREAMS - EARLY, 7, CHUNK, COLS), BF),
            vmem((STREAMS, CHUNK, COLS), F32),
            vmem((STREAMS, GROUP, COLS), BF),
            vmem((STREAMS, GROUP, COLS), BF),
            vmem((EARLY, 8, GROUP, COLS), BF),
            vmem((EARLY, 8, GROUP, COLS), BF),
            vmem((EARLY, 7, GROUP, COLS), BF),
            vmem((EARLY, 7, GROUP, COLS), BF),
            vmem((EARLY, 8, GROUP, COLS), F32),
            dma((5,)),
            dma((128,)), dma((96,)),
            dma((3,)), dma((4,)),
            dma((3,)), dma((4,)),
            dma((3,)), dma((4,)),
            dma((7,)), dma((8,)),
            dma((15,)), dma((16,)),
            dma((1,)), dma((2,)),
            dma((STREAMS, 7)), dma((STREAMS, 7)),
            dma((STREAMS,)), dma((STREAMS,)),
        ],
        compiler_params=pltpu.CompilerParams(
            collective_id=0, has_side_effects=True, vmem_limit_bytes=63 * 1024 * 1024
        ),
        cost_estimate=pl.CostEstimate(flops=4 * ROWS * WIDTH * SLICE, bytes_accessed=4 * 1024 * 1024, transcendentals=3 * ROWS * SLICE),
    )(hidden, head_weight, head_bias.reshape(1, SLICE), lengths, positives)


def solution(mesh):
    return jax.shard_map(
        per_device,
        mesh=mesh,
        in_specs=(P("dp", None), P("dp", "vocab"), P("vocab"), P("dp", None), P("dp")),
        out_specs=P(("dp", "vocab"), None),
        check_vma=False,
    )
```

```python
import jax
import jax.numpy as jnp
from jax import lax
from jax.experimental import pallas as pl
from jax.experimental.pallas import tpu as pltpu
from jax.sharding import PartitionSpec as P

QLEN = 32
PLEN = 80
ROWS_PAIR = QLEN + PLEN
ROWS = 2 * ROWS_PAIR
WIDTH = 4096
SLICE = 1024
SHARD = 128
PAIRS = 64

POOL_TEMP = 0.25
SCORE_TEMP = 0.01
LOSS_SCALE = 65536.0
SCORE_SCALE = 1.0 / (SCORE_TEMP * 16384)

GROUP = 16
OWN = 14
CHUNK = 2 * GROUP
STREAMS = 8
COLS = WIDTH // STREAMS
EARLY = 1
LAG = 8

BF = jnp.bfloat16
F32 = jnp.float32
MESH = pl.DeviceIdType.MESH

SEGMENTS = (
    (0, QLEN),
    (ROWS_PAIR, QLEN),
    (QLEN, PLEN),
    (ROWS_PAIR + QLEN, PLEN),
)


def kernel(
    hidden_ref, weight_ref, bias_hbm, lengths_hbm, positives_hbm, out_ref,
    bias_ref, lengths_ref, positives_ref, hid, wf, act, sums, vecs, packed, pooled, select, spread, both, twice, part_scores, score_parts,
    grads, grads_t, targets, row_targets, lgrad, part, chain_out, chain_in, kept, swap_out, swap_in,
    wide_out, wide_in, near_out, near_in, summed,
    local_sem, w_send, w_recv, t_send, t_recv, u_send, u_recv, v_send, v_recv, g_send, g_recv,
    s_send, s_recv, d_send, d_recv, c_send, c_recv, y_send, y_recv, plane_sem, vocab_sem, last_sem,
):
    dp = lax.axis_index("dp")
    vocab = lax.axis_index("vocab")
    x, y, core = dp // 8, (dp // 2) % 4, dp % 2
    z, hi = vocab // 2, vocab % 2
    xc = core * 4 + x

    def dp_of(xx, yy, cc):
        return (xx * 4 + yy) * 2 + cc

    load_w = pltpu.make_async_copy(weight_ref, wf.at[pl.ds(pl.multiple_of(dp * SHARD, SHARD), SHARD)], local_sem.at[0])
    load_h = pltpu.make_async_copy(hidden_ref, hid, local_sem.at[1])
    loads = [
        load_w,
        load_h,
        pltpu.make_async_copy(bias_hbm, bias_ref, local_sem.at[2]),
        pltpu.make_async_copy(lengths_hbm, lengths_ref, local_sem.at[3]),
        pltpu.make_async_copy(positives_hbm, positives_ref, local_sem.at[4]),
    ]
    for load in loads:
        load.start()

    y_peers = [dp_of(x, (y + o) % 4, core) for o in range(1, 4)]
    xc_peers = [(xc + o) % 8 for o in range(1, 8)]
    xc_dp = [dp_of(p % 4, y, p // 4) for p in xc_peers]
    vocab_peers = [(vocab + o) % 16 for o in range(1, 16)]

    right, left, far = (x + 1) % 4, (x + 3) % 4, (x + 2) % 4
    to_right, to_left = dp_of(right, y, core), dp_of(left, y, core)
    above, below = dp_of(x, jnp.minimum(y + 1, 3), core), dp_of(x, jnp.maximum(y - 1, 0), core)
    sibling = dp_of(x, y, 1 - core)
    white = (x + y + core + z + hi) % 2 == 1
    black = jnp.logical_not(white)
    others = [((z + o) % 8) * 2 + (1 - hi if o % 2 == 0 else hi) for o in range(8)]
    plane_count = jnp.where((y == 0) | (y == 3), 4, 5)
    barrier = pltpu.get_barrier_semaphore()

    def greet(sem, to_dp, to_vocab):
        pl.semaphore_signal(sem, inc=1, device_id={"dp": to_dp, "vocab": to_vocab}, device_id_type=MESH)

    def greet_plane(sem):
        for p in (to_right, to_left, sibling):
            greet(sem, p, vocab)
        pl.when(y < 3)(lambda: greet(sem, above, vocab))
        pl.when(y > 0)(lambda: greet(sem, below, vocab))

    def greet_others(sem):
        for p in others:
            greet(sem, dp, p)

    pl.when(white)(lambda: greet_plane(barrier))
    pl.when(black)(lambda: greet_others(barrier))

    @pl.when(black)
    def _():
        pl.semaphore_wait(barrier, plane_count)
        greet_plane(plane_sem)

    @pl.when(white)
    def _():
        pl.semaphore_wait(plane_sem, plane_count)

    def others_answer():
        @pl.when(white)
        def _():
            pl.semaphore_wait(barrier, 8)
            greet_others(vocab_sem)

    def others_known():
        @pl.when(black)
        def _():
            pl.semaphore_wait(vocab_sem, 8)
            greet(last_sem, dp, z * 2 + 1 - hi)

    def all_known():
        @pl.when(white)
        def _():
            pl.semaphore_wait(last_sem, 1)

    load_w.wait()

    sends = []
    copies = []

    def remote(src, dst, send_sem, recv_sem, to_dp, to_vocab):
        copy = pltpu.make_async_remote_copy(
            src_ref=src, dst_ref=dst, send_sem=send_sem, recv_sem=recv_sem,
            device_id={"dp": to_dp, "vocab": to_vocab}, device_id_type=MESH,
        )
        copy.start()
        copies.append(copy)

    UNITS = ((0, 64), (64, 48), (112, 16))
    FIRST, REST = (0, 1), 2

    def unit(slot, u):
        start, size = UNITS[u]
        return wf.at[pl.ds(pl.multiple_of(slot * SHARD + start, 16), size)]

    def w_sem(slot, u):
        return w_recv.at[slot * 3 + u]

    def arrived(slot, u):
        pltpu.make_async_copy(unit(slot, u), unit(slot, u), w_sem(slot, u)).wait()

    count = [0]

    def send(slot, u, to, cond=None):
        n = count[0]
        count[0] += 1
        copy = pltpu.make_async_remote_copy(
            src_ref=unit(slot, u), dst_ref=unit(slot, u), send_sem=w_send.at[n], recv_sem=w_sem(slot, u),
            device_id={"dp": to, "vocab": vocab}, device_id_type=MESH,
        )
        if cond is None:
            copy.start()
        else:
            pl.when(cond)(copy.start)
        sends.append((cond, copy))

    def line_place(t):
        low = jnp.where(y < 2, y, 3 - y)
        place = jnp.where((low == 1) & (t < 2), 1 - t, t)
        return jnp.where(y < 2, place, 3 - place)

    def onward(slot, u, yy):
        rising = yy < y
        send(slot, u, jnp.where(rising, above, below), (rising & (y < 3)) | ((yy > y) & (y > 0)))

    def both_ways(slot, u):
        send(slot, u, above, y < 3)
        send(slot, u, below, y > 0)

    def column(t):
        yy = line_place(t)
        slot = dp_of(x, yy, core)
        for u in FIRST:
            if t == 0:
                both_ways(slot, u)
            else:
                arrived(slot, u)
                onward(slot, u, yy)
            send(slot, u, to_right)
            send(slot, u, to_left)
            send(slot, u, sibling)

    def relay(u, yy):
        rightward = (yy + u) % 2 == 0
        slot = dp_of(jnp.where(rightward, left, right), yy, core)
        arrived(slot, u)
        send(slot, u, jnp.where(rightward, to_right, to_left))
        send(slot, u, sibling)
        slot = dp_of(jnp.where(rightward, right, left), yy, core)
        arrived(slot, u)
        send(slot, u, sibling)

    def neighbours(t):
        for u in FIRST:
            relay(u, line_place(t))

    def last(t):
        slot = dp_of(far, line_place(t), core)
        for u in FIRST:
            arrived(slot, u)
            send(slot, u, sibling)

    def rest_own():
        send(dp, REST, to_right)
        send(dp, REST, to_left)
        send(dp, REST, sibling)

    def rest_neighbours():
        relay(REST, y)

    def rest_out():
        for source in (x, left, right):
            both_ways(dp_of(source, y, core), REST)

    def rest_last():
        slot = dp_of(far, y, core)
        arrived(slot, REST)
        both_ways(slot, REST)
        send(slot, REST, sibling)

    def rest_line(t):
        yy = line_place(t)
        for source in (x, left, right, far):
            slot = dp_of(source, yy, core)
            arrived(slot, REST)
            onward(slot, REST, yy)
            send(slot, REST, sibling)

    def dots(t):
        yy = line_place(t)

        def step(i, carry):
            chip = ((x + 3 + i) % 4) * 4 + yy
            for u in FIRST + (REST,):
                arrived(chip * 2 + 1 - core, u)
            deep = pl.ds(pl.multiple_of(chip * 256, 256), 256)
            act[...] += jnp.dot(hid[:, deep], wf[deep, :], preferred_element_type=F32)
            return carry

        lax.fori_loop(0, 4, step, 0)

    column(0)
    rest_own()

    for load in loads[1:]:
        load.wait()

    row = lax.broadcasted_iota(jnp.int32, (128, 512), 0)
    col = lax.broadcasted_iota(jnp.int32, (128, 512), 1)
    pair = row % PAIRS
    first = (pair // 2) * 16 + pair % 2 + jnp.where(row < PAIRS, 2, 0)
    for i in range(4):
        select[i] = jnp.where(col == first + 4 * i, 1.0, 0.0).astype(BF)
    prow = lax.broadcasted_iota(jnp.int32, (256, 256), 0)
    pcol = lax.broadcasted_iota(jnp.int32, (256, 256), 1)
    wanted = (prow // GROUP) * OWN + prow % GROUP
    spread[...] = jnp.where((pcol == wanted) & (prow % GROUP < OWN), 1.0, 0.0).astype(BF)
    lgrad[pl.ds(ROWS, 32), :] = jnp.zeros((32, SLICE), BF)
    act[...] = jnp.broadcast_to(bias_ref[...], (ROWS, SLICE))

    trow = lax.broadcasted_iota(jnp.int32, (8, 128), 0)
    tcol = lax.broadcasted_iota(jnp.int32, (8, 128), 1)
    tile = jnp.zeros((8, 128), F32)
    for j in range(2):
        k = positives_ref[j]
        place = ((k // 2) % 2) * 32 + (k // 16) * 8 + ((k // 4) % 4) * 2 + k % 2
        tile = tile + jnp.where((trow == 2 * y + j) & (tcol == place), 1.0, 0.0)
    targets[y] = tile

    column(1)
    neighbours(0)
    column(2)
    rest_neighbours()
    neighbours(1)
    others_answer()
    column(3)
    rest_out()
    for i, p in enumerate(y_peers):
        remote(targets.at[y], targets.at[y], t_send.at[i], t_recv.at[y], p, vocab)
    last(0)
    rest_last()
    neighbours(2)
    rest_line(1)
    last(1)
    neighbours(3)
    rest_line(2)
    last(2)
    for o in range(1, 4):
        yy = (y + o) % 4
        pltpu.make_async_copy(targets.at[yy], targets.at[yy], t_recv.at[yy]).wait()
    row_targets[x] = targets[0] + targets[1] + targets[2] + targets[3]
    for i, p in enumerate((right, left, far)):
        remote(row_targets.at[x], row_targets.at[x], u_send.at[i], u_recv.at[x], dp_of(p, y, core), vocab)
    rest_line(3)
    last(3)
    others_known()
    for t in range(4):
        dots(t)
    for o in range(1, 4):
        block = row_targets.at[(x + o) % 4]
        pltpu.make_async_copy(block, block, u_recv.at[(x + o) % 4]).wait()

    def pool(b, carry):
        cols = pl.ds(pl.multiple_of(b * 128, 128), 128)
        for n, (start, size) in enumerate(SEGMENTS):
            length = lengths_ref[n % 2, n // 2]
            logits = act[pl.ds(start, size), cols]
            position = lax.broadcasted_iota(jnp.int32, (size, 128), 0)
            mask = jnp.where(position < length, 1.0, 0.0).astype(F32)
            small = jnp.exp(-jnp.abs(logits))
            above = 1.0 + jnp.maximum(logits, 0.0) + jnp.log1p(small)
            slope = jnp.where(logits >= 0.0, 1.0, small) / (1.0 + small)
            cubed = mask * (above * above * above)
            total = jnp.sum(cubed * above, axis=0, keepdims=True)
            act[pl.ds(start, size), cols] = cubed * slope
            sums[pl.ds(n, 1), cols] = total
            vecs[pl.ds(n, 1), cols] = POOL_TEMP * jnp.log(total / length.astype(F32))
        return carry

    lax.fori_loop(0, 8, pool, 0)
    for i in range(4):
        packed[pl.ds(4 * i, 4), :] = vecs[pl.ds(0, 4), pl.ds(256 * i, 256)]
    mine = xc * 4 + y
    pooled[mine] = packed[...].astype(BF)

    for i, p in enumerate(y_peers):
        remote(pooled.at[mine], pooled.at[mine], v_send.at[i], v_recv.at[y], p, vocab)
    for o in range(1, 4):
        yy = (y + o) % 4
        pltpu.make_async_copy(pooled.at[xc * 4 + yy], pooled.at[xc * 4 + yy], v_recv.at[yy]).wait()
    line = pl.ds(xc * 4, 4)
    for i, p in enumerate(xc_dp):
        remote(pooled.at[line], pooled.at[line], g_send.at[i], g_recv.at[xc], p, vocab)
    for p in xc_peers:
        block = pooled.at[pl.ds(p * 4, 4)]
        pltpu.make_async_copy(block, block, g_recv.at[p]).wait()

    flat = pooled[...].reshape(512, 256)
    for i in range(4):
        both[:, pl.ds(256 * i, 256)] = jnp.dot(select[i], flat, preferred_element_type=F32).astype(BF)
    passages = both[pl.ds(0, PAIRS), :]
    twice[pl.ds(0, PAIRS), :] = passages
    twice[pl.ds(PAIRS, PAIRS), :] = passages
    nt = (((1,), (1,)), ((), ()))
    part_scores[...] = lax.dot_general(both[pl.ds(PAIRS, PAIRS), :], twice[...], nt, preferred_element_type=F32)

    rows8 = pl.ds(pl.multiple_of(xc * 8, 8), 8)
    low_lanes = lax.broadcasted_iota(jnp.int32, (16, 128), 1) < PAIRS
    first_rows = pl.ds(pl.multiple_of(core * 32, 16), 16)
    next_rows = pl.ds(pl.multiple_of(core * 32 + 16, 16), 16)
    score_parts[vocab] = jnp.where(low_lanes, part_scores[first_rows, :], part_scores[next_rows, :])
    all_known()
    for i, p in enumerate(vocab_peers):
        remote(score_parts.at[vocab], score_parts.at[vocab], s_send.at[i], s_recv.at[vocab], dp, p)
    for p in vocab_peers:
        pltpu.make_async_copy(score_parts.at[p], score_parts.at[p], s_recv.at[p]).wait()
    summed_parts = jnp.sum(score_parts[...], axis=0)
    scores = SCORE_SCALE * jnp.concatenate([summed_parts, pltpu.roll(summed_parts, PAIRS, 1)], axis=0)
    valid = lax.broadcasted_iota(jnp.int32, (32, 128), 1) < PAIRS
    top = jnp.max(jnp.where(valid, scores, -jnp.inf), axis=1, keepdims=True)
    shifted = jnp.where(valid, jnp.exp(jnp.where(valid, scores - top, 0.0)), 0.0)
    soft = shifted / jnp.sum(shifted, axis=1, keepdims=True)
    grads[pl.ds(core, 1)] = (LOSS_SCALE * (soft - row_targets[...].reshape(32, 128))).reshape(1, 32, 128)
    remote(grads.at[core], grads.at[core], d_send.at[0], d_recv.at[core], sibling, vocab)
    pltpu.make_async_copy(grads.at[1 - core], grads.at[1 - core], d_recv.at[1 - core]).wait()
    whole = jnp.concatenate([grads[...].reshape(PAIRS, 128), jnp.zeros((PAIRS, 128), F32)], axis=0)
    grads_t[...] = whole.T

    def exact_dot(lhs, rhs):
        a = lhs.astype(BF)
        rest = lhs - a.astype(F32)
        b = rest.astype(BF)
        c = (rest - b.astype(F32)).astype(BF)
        out = jnp.dot(c, rhs, preferred_element_type=F32)
        out = out + jnp.dot(b, rhs, preferred_element_type=F32)
        return out + jnp.dot(a, rhs, preferred_element_type=F32)

    rows8_here = pl.ds(pl.multiple_of(x * 8, 8), 8)
    q_grad = exact_dot(grads[core, rows8_here, :][:, :PAIRS], both[pl.ds(0, PAIRS), :])
    p_grad = exact_dot(grads_t[rows8, :][:, :PAIRS], both[pl.ds(PAIRS, PAIRS), :])
    srow = lax.broadcasted_iota(jnp.int32, (8, SLICE), 0)
    for n, (start, size) in enumerate(SEGMENTS):
        grad = q_grad if n < 2 else p_grad
        one = jnp.sum(jnp.where(srow == 2 * y + n % 2, grad, 0.0), axis=0, keepdims=True)
        vecs[pl.ds(n, 1), :] = (SCORE_SCALE * one) / sums[pl.ds(n, 1), :]

    def finish(b, carry):
        cols = pl.ds(pl.multiple_of(b * 128, 128), 128)
        for n, (start, size) in enumerate(SEGMENTS):
            lgrad[pl.ds(start, size), cols] = (act[pl.ds(start, size), cols] * vecs[pl.ds(n, 1), cols]).astype(BF)
        return carry

    lax.fori_loop(0, 8, finish, 0)
    lgrad[...] = jnp.dot(spread[...], lgrad[...], preferred_element_type=F32).astype(BF)

    up, down = ((z + 1) % 8) * 2 + hi, ((z + 7) % 8) * 2 + hi
    across = z * 2 + 1 - hi

    def cols_of(c):
        return pl.ds(c * COLS, COLS)

    def own_part(c, k):
        place = (z + k + 8) % 8
        if c < EARLY:
            return summed[c, place]
        return part[pl.ds(pl.multiple_of(place * CHUNK, CHUNK), CHUNK), cols_of(c)]

    def hop(c, i, value, to):
        if c < EARLY:
            out_slot, in_slot = near_out.at[c, i], near_in.at[c, i]
        else:
            out_slot, in_slot = chain_out.at[c - EARLY, i], chain_in.at[c - EARLY, i]
        out_slot[...] = value.astype(BF)
        remote(out_slot, in_slot, c_send.at[c, i], c_recv.at[c, i], dp, to)

    def landed(c, i):
        in_slot = near_in.at[c, i] if c < EARLY else chain_in.at[c - EARLY, i]
        pltpu.make_async_copy(in_slot, in_slot, c_recv.at[c, i]).wait()
        return in_slot[...].astype(F32)

    def chain(c, s):
        a = 4 if c % 2 == 0 else 3
        b = 7 - a
        if s == 0:
            hop(c, 0, own_part(c, a), up)
            hop(c, a, own_part(c, -b), down)
        elif s < 4:
            if s < a:
                hop(c, s, landed(c, s - 1) + own_part(c, a - s), up)
            if s < b:
                hop(c, a + s, landed(c, a + s - 1) + own_part(c, s - b), down)
        else:
            return own_part(c, 0) + landed(c, a - 1) + landed(c, 6)

    def product(c):
        part[:, cols_of(c)] = lax.dot_general(lgrad[...], wf[cols_of(c), :], nt, preferred_element_type=F32)

    def group(c, place, h):
        return part[pl.ds(pl.multiple_of(place * CHUNK + h * GROUP, GROUP), GROUP), cols_of(c)]

    def early(c, s):
        if s == 0:
            product(c)
            for place in range(8):
                wide_out[c, place] = group(c, place, 1 - hi).astype(BF)
            remote(wide_out.at[c], wide_in.at[c], y_send.at[c], y_recv.at[c], dp, across)
        elif s == 1:
            pltpu.make_async_copy(wide_in.at[c], wide_in.at[c], y_recv.at[c]).wait()
            for place in range(8):
                summed[c, place] = group(c, place, hi) + wide_in[c, place].astype(F32)
            chain(c, 0)
        elif s < 5:
            chain(c, s - 1)
        else:
            out_ref[:, cols_of(c)] = chain(c, 4)[:OWN].astype(BF)

    def late(c, s):
        if s == 0:
            product(c)
        if s < 4:
            chain(c, s)
        elif s == 4:
            kept[c] = chain(c, 4)
            swap_out[c] = kept[c, pl.ds(pl.multiple_of((1 - hi) * GROUP, GROUP), GROUP), :].astype(BF)
            remote(swap_out.at[c], swap_in.at[c], y_send.at[c], y_recv.at[c], dp, across)
        else:
            pltpu.make_async_copy(swap_in.at[c], swap_in.at[c], y_recv.at[c]).wait()
            total = kept[c, pl.ds(pl.multiple_of(hi * GROUP, GROUP), GROUP), :] + swap_in[c].astype(F32)
            out_ref[:, cols_of(c)] = total[:OWN].astype(BF)

    def when(c, s):
        if c < EARLY:
            return (STREAMS * s + c + (LAG if s else 0), c)
        return (STREAMS * s + c, c)

    for c, s in sorted(((c, s) for c in range(STREAMS) for s in range(6)), key=lambda e: when(*e)):
        (early if c < EARLY else late)(c, s)

    for cond, copy in sends:
        if cond is None:
            copy.wait_send()
        else:
            pl.when(cond)(copy.wait_send)
    for copy in copies:
        copy.wait_send()


def per_device(hidden, head_weight, head_bias, lengths, positives):
    vmem, smem = pltpu.VMEM, pltpu.SMEM
    dma = pltpu.SemaphoreType.DMA
    return pl.pallas_call(
        kernel,
        out_shape=jax.ShapeDtypeStruct((OWN, WIDTH), BF),
        in_specs=[
            pl.BlockSpec(memory_space=pl.ANY),
            pl.BlockSpec(memory_space=pl.ANY),
            pl.BlockSpec(memory_space=pl.ANY),
            pl.BlockSpec(memory_space=pl.ANY),
            pl.BlockSpec(memory_space=pl.ANY),
        ],
        out_specs=pl.BlockSpec(memory_space=vmem),
        scratch_shapes=[
            vmem((1, SLICE), F32),
            smem((2, 2), jnp.int32),
            smem((2,), jnp.int32),
            vmem((ROWS, WIDTH), BF),
            vmem((WIDTH, SLICE), BF),
            vmem((ROWS, SLICE), F32),
            vmem((8, SLICE), F32),
            vmem((8, SLICE), F32),
            vmem((16, 256), F32),
            vmem((32, 16, 256), BF),
            vmem((4, 128, 512), BF),
            vmem((256, 256), BF),
            vmem((128, SLICE), BF),
            vmem((128, SLICE), BF),
            vmem((PAIRS, 128), F32),
            vmem((16, 16, 128), F32),
            vmem((2, 32, 128), F32),
            vmem((128, 128), F32),
            vmem((4, 8, 128), F32),
            vmem((4, 8, 128), F32),
            vmem((256, SLICE), BF),
            vmem((256, WIDTH), F32),
            vmem((STREAMS - EARLY, 7, CHUNK, COLS), BF),
            vmem((STREAMS - EARLY, 7, CHUNK, COLS), BF),
            vmem((STREAMS, CHUNK, COLS), F32),
            vmem((STREAMS, GROUP, COLS), BF),
            vmem((STREAMS, GROUP, COLS), BF),
            vmem((EARLY, 8, GROUP, COLS), BF),
            vmem((EARLY, 8, GROUP, COLS), BF),
            vmem((EARLY, 7, GROUP, COLS), BF),
            vmem((EARLY, 7, GROUP, COLS), BF),
            vmem((EARLY, 8, GROUP, COLS), F32),
            dma((5,)),
            dma((128,)), dma((96,)),
            dma((3,)), dma((4,)),
            dma((3,)), dma((4,)),
            dma((3,)), dma((4,)),
            dma((7,)), dma((8,)),
            dma((15,)), dma((16,)),
            dma((1,)), dma((2,)),
            dma((STREAMS, 7)), dma((STREAMS, 7)),
            dma((STREAMS,)), dma((STREAMS,)),
            pltpu.SemaphoreType.REGULAR, pltpu.SemaphoreType.REGULAR, pltpu.SemaphoreType.REGULAR,
        ],
        compiler_params=pltpu.CompilerParams(
            collective_id=0, has_side_effects=True, vmem_limit_bytes=63 * 1024 * 1024
        ),
        cost_estimate=pl.CostEstimate(flops=4 * ROWS * WIDTH * SLICE, bytes_accessed=4 * 1024 * 1024, transcendentals=3 * ROWS * SLICE),
    )(hidden, head_weight, head_bias.reshape(1, SLICE), lengths, positives)


def solution(mesh):
    return jax.shard_map(
        per_device,
        mesh=mesh,
        in_specs=(P("dp", None), P("dp", "vocab"), P("vocab"), P("dp", None), P("dp")),
        out_specs=P(("dp", "vocab"), None),
        check_vma=False,
    )
```

```python
import jax
import jax.numpy as jnp
from jax import lax
from jax.experimental import pallas as pl
from jax.experimental.pallas import tpu as pltpu
from jax.sharding import PartitionSpec as P

QLEN = 32
PLEN = 80
ROWS_PAIR = QLEN + PLEN
ROWS = 2 * ROWS_PAIR
WIDTH = 4096
SLICE = 1024
SHARD = 128
PAIRS = 64

POOL_TEMP = 0.25
SCORE_TEMP = 0.01
LOSS_SCALE = 65536.0
SCORE_SCALE = 1.0 / (SCORE_TEMP * 16384)

GROUP = 16
OWN = 14
CHUNK = 2 * GROUP
STREAMS = 8
COLS = WIDTH // STREAMS
EARLY = 1
LAG = 8

BF = jnp.bfloat16
F32 = jnp.float32
MESH = pl.DeviceIdType.MESH

SEGMENTS = (
    (0, QLEN),
    (ROWS_PAIR, QLEN),
    (QLEN, PLEN),
    (ROWS_PAIR + QLEN, PLEN),
)


def kernel(
    hidden_ref, weight_ref, bias_hbm, lengths_hbm, positives_hbm, out_ref,
    bias_ref, lengths_ref, positives_ref, hid, wf, act, sums, vecs, packed, pooled, select, spread, both, twice, part_scores, score_parts,
    grads, grads_t, targets, row_targets, lgrad, part, chain_out, chain_in, kept, swap_out, swap_in,
    wide_out, wide_in, near_out, near_in, summed,
    local_sem, w_send, w_recv, t_send, t_recv, u_send, u_recv, v_send, v_recv, g_send, g_recv,
    s_send, s_recv, d_send, d_recv, c_send, c_recv, y_send, y_recv, plane_sem, vocab_sem, last_sem,
):
    dp = lax.axis_index("dp")
    vocab = lax.axis_index("vocab")
    x, y, core = dp // 8, (dp // 2) % 4, dp % 2
    z, hi = vocab // 2, vocab % 2
    xc = core * 4 + x

    def dp_of(xx, yy, cc):
        return (xx * 4 + yy) * 2 + cc

    load_w = pltpu.make_async_copy(weight_ref, wf.at[pl.ds(pl.multiple_of(dp * SHARD, SHARD), SHARD)], local_sem.at[0])
    load_h = pltpu.make_async_copy(hidden_ref, hid, local_sem.at[1])
    loads = [
        load_w,
        load_h,
        pltpu.make_async_copy(bias_hbm, bias_ref, local_sem.at[2]),
        pltpu.make_async_copy(lengths_hbm, lengths_ref, local_sem.at[3]),
        pltpu.make_async_copy(positives_hbm, positives_ref, local_sem.at[4]),
    ]
    for load in loads:
        load.start()

    y_peers = [dp_of(x, (y + o) % 4, core) for o in range(1, 4)]
    xc_peers = [(xc + o) % 8 for o in range(1, 8)]
    xc_dp = [dp_of(p % 4, y, p // 4) for p in xc_peers]
    vocab_peers = [(vocab + o) % 16 for o in range(1, 16)]

    right, left, far = (x + 1) % 4, (x + 3) % 4, (x + 2) % 4
    to_right, to_left = dp_of(right, y, core), dp_of(left, y, core)
    above, below = dp_of(x, jnp.minimum(y + 1, 3), core), dp_of(x, jnp.maximum(y - 1, 0), core)
    sibling = dp_of(x, y, 1 - core)
    white = (x + y + core + z + hi) % 2 == 1
    black = jnp.logical_not(white)
    others = [((z + o) % 8) * 2 + (1 - hi if o % 2 == 0 else hi) for o in range(8)]
    plane_count = jnp.where((y == 0) | (y == 3), 4, 5)
    barrier = pltpu.get_barrier_semaphore()

    def greet(sem, to_dp, to_vocab):
        pl.semaphore_signal(sem, inc=1, device_id={"dp": to_dp, "vocab": to_vocab}, device_id_type=MESH)

    def greet_plane(sem):
        for p in (to_right, to_left, sibling):
            greet(sem, p, vocab)
        pl.when(y < 3)(lambda: greet(sem, above, vocab))
        pl.when(y > 0)(lambda: greet(sem, below, vocab))

    def greet_others(sem):
        for p in others:
            greet(sem, dp, p)

    pl.when(white)(lambda: greet_plane(barrier))
    pl.when(black)(lambda: greet_others(barrier))

    @pl.when(black)
    def _():
        pl.semaphore_wait(barrier, plane_count)
        greet_plane(plane_sem)

    @pl.when(white)
    def _():
        pl.semaphore_wait(plane_sem, plane_count)

    def others_answer():
        @pl.when(white)
        def _():
            pl.semaphore_wait(barrier, 8)
            greet_others(vocab_sem)

    def others_known():
        @pl.when(black)
        def _():
            pl.semaphore_wait(vocab_sem, 8)
            greet(last_sem, dp, z * 2 + 1 - hi)

    def all_known():
        @pl.when(white)
        def _():
            pl.semaphore_wait(last_sem, 1)

    load_w.wait()

    sends = []
    copies = []

    def remote(src, dst, send_sem, recv_sem, to_dp, to_vocab):
        copy = pltpu.make_async_remote_copy(
            src_ref=src, dst_ref=dst, send_sem=send_sem, recv_sem=recv_sem,
            device_id={"dp": to_dp, "vocab": to_vocab}, device_id_type=MESH,
        )
        copy.start()
        copies.append(copy)

    UNITS = ((0, 64), (64, 48), (112, 16))
    FIRST, REST = (0, 1), 2

    def unit(slot, u):
        start, size = UNITS[u]
        return wf.at[pl.ds(pl.multiple_of(slot * SHARD + start, 16), size)]

    def w_sem(slot, u):
        return w_recv.at[slot * 3 + u]

    def arrived(slot, u):
        pltpu.make_async_copy(unit(slot, u), unit(slot, u), w_sem(slot, u)).wait()

    count = [0]

    def send(slot, u, to, cond=None):
        n = count[0]
        count[0] += 1
        copy = pltpu.make_async_remote_copy(
            src_ref=unit(slot, u), dst_ref=unit(slot, u), send_sem=w_send.at[n], recv_sem=w_sem(slot, u),
            device_id={"dp": to, "vocab": vocab}, device_id_type=MESH,
        )
        if cond is None:
            copy.start()
        else:
            pl.when(cond)(copy.start)
        sends.append((cond, copy))

    def line_place(t):
        low = jnp.where(y < 2, y, 3 - y)
        place = jnp.where((low == 1) & (t < 2), 1 - t, t)
        return jnp.where(y < 2, place, 3 - place)

    def onward(slot, u, yy):
        rising = yy < y
        send(slot, u, jnp.where(rising, above, below), (rising & (y < 3)) | ((yy > y) & (y > 0)))

    def both_ways(slot, u):
        send(slot, u, above, y < 3)
        send(slot, u, below, y > 0)

    def column(t):
        yy = line_place(t)
        slot = dp_of(x, yy, core)
        for u in FIRST:
            if t == 0:
                both_ways(slot, u)
            else:
                arrived(slot, u)
                onward(slot, u, yy)
            send(slot, u, to_right)
            send(slot, u, to_left)
            send(slot, u, sibling)

    def relay(u, yy):
        rightward = (yy + u) % 2 == 0
        slot = dp_of(jnp.where(rightward, left, right), yy, core)
        arrived(slot, u)
        send(slot, u, jnp.where(rightward, to_right, to_left))
        send(slot, u, sibling)
        slot = dp_of(jnp.where(rightward, right, left), yy, core)
        arrived(slot, u)
        send(slot, u, sibling)

    def neighbours(t):
        for u in FIRST:
            relay(u, line_place(t))

    def last(t):
        slot = dp_of(far, line_place(t), core)
        for u in FIRST:
            arrived(slot, u)
            send(slot, u, sibling)

    def rest_own():
        send(dp, REST, to_right)
        send(dp, REST, to_left)
        send(dp, REST, sibling)

    def rest_neighbours():
        relay(REST, y)

    def rest_out():
        for source in (x, left, right):
            both_ways(dp_of(source, y, core), REST)

    def rest_last():
        slot = dp_of(far, y, core)
        arrived(slot, REST)
        both_ways(slot, REST)
        send(slot, REST, sibling)

    def rest_line(t):
        yy = line_place(t)
        for source in (x, left, right, far):
            slot = dp_of(source, yy, core)
            arrived(slot, REST)
            onward(slot, REST, yy)
            send(slot, REST, sibling)

    def dots(t):
        yy = line_place(t)

        def step(i, carry):
            chip = ((x + 3 + i) % 4) * 4 + yy
            for u in FIRST + (REST,):
                arrived(chip * 2 + 1 - core, u)
            deep = pl.ds(pl.multiple_of(chip * 256, 256), 256)
            act[...] += jnp.dot(hid[:, deep], wf[deep, :], preferred_element_type=F32)
            return carry

        lax.fori_loop(0, 4, step, 0)

    column(0)
    rest_own()

    for load in loads[1:]:
        load.wait()

    row = lax.broadcasted_iota(jnp.int32, (128, 512), 0)
    col = lax.broadcasted_iota(jnp.int32, (128, 512), 1)
    pair = row % PAIRS
    first = (pair // 2) * 16 + pair % 2 + jnp.where(row < PAIRS, 2, 0)
    for i in range(4):
        select[i] = jnp.where(col == first + 4 * i, 1.0, 0.0).astype(BF)
    prow = lax.broadcasted_iota(jnp.int32, (256, 256), 0)
    pcol = lax.broadcasted_iota(jnp.int32, (256, 256), 1)
    wanted = (prow // GROUP) * OWN + prow % GROUP
    spread[...] = jnp.where((pcol == wanted) & (prow % GROUP < OWN), 1.0, 0.0).astype(BF)
    lgrad[pl.ds(ROWS, 32), :] = jnp.zeros((32, SLICE), BF)
    act[...] = jnp.broadcast_to(bias_ref[...], (ROWS, SLICE))

    trow = lax.broadcasted_iota(jnp.int32, (8, 128), 0)
    tcol = lax.broadcasted_iota(jnp.int32, (8, 128), 1)
    tile = jnp.zeros((8, 128), F32)
    for j in range(2):
        k = positives_ref[j]
        place = ((k // 2) % 2) * 32 + (k // 16) * 8 + ((k // 4) % 4) * 2 + k % 2
        tile = tile + jnp.where((trow == 2 * y + j) & (tcol == place), 1.0, 0.0)
    targets[y] = tile

    column(1)
    neighbours(0)
    column(2)
    rest_neighbours()
    neighbours(1)
    column(3)
    rest_out()
    for i, p in enumerate(y_peers):
        remote(targets.at[y], targets.at[y], t_send.at[i], t_recv.at[y], p, vocab)
    last(0)
    rest_last()
    others_answer()
    neighbours(2)
    rest_line(1)
    last(1)
    neighbours(3)
    rest_line(2)
    last(2)
    for o in range(1, 4):
        yy = (y + o) % 4
        pltpu.make_async_copy(targets.at[yy], targets.at[yy], t_recv.at[yy]).wait()
    row_targets[x] = targets[0] + targets[1] + targets[2] + targets[3]
    for i, p in enumerate((right, left, far)):
        remote(row_targets.at[x], row_targets.at[x], u_send.at[i], u_recv.at[x], dp_of(p, y, core), vocab)
    dots(0)
    dots(1)
    rest_line(3)
    last(3)
    others_known()
    dots(2)
    dots(3)
    for o in range(1, 4):
        block = row_targets.at[(x + o) % 4]
        pltpu.make_async_copy(block, block, u_recv.at[(x + o) % 4]).wait()

    def pool(b, carry):
        cols = pl.ds(pl.multiple_of(b * 128, 128), 128)
        for n, (start, size) in enumerate(SEGMENTS):
            length = lengths_ref[n % 2, n // 2]
            logits = act[pl.ds(start, size), cols]
            position = lax.broadcasted_iota(jnp.int32, (size, 128), 0)
            mask = jnp.where(position < length, 1.0, 0.0).astype(F32)
            small = jnp.exp(-jnp.abs(logits))
            above = 1.0 + jnp.maximum(logits, 0.0) + jnp.log1p(small)
            slope = jnp.where(logits >= 0.0, 1.0, small) / (1.0 + small)
            cubed = mask * (above * above * above)
            total = jnp.sum(cubed * above, axis=0, keepdims=True)
            act[pl.ds(start, size), cols] = cubed * slope
            sums[pl.ds(n, 1), cols] = total
            vecs[pl.ds(n, 1), cols] = POOL_TEMP * jnp.log(total / length.astype(F32))
        return carry

    lax.fori_loop(0, 8, pool, 0)
    for i in range(4):
        packed[pl.ds(4 * i, 4), :] = vecs[pl.ds(0, 4), pl.ds(256 * i, 256)]
    mine = xc * 4 + y
    pooled[mine] = packed[...].astype(BF)

    for i, p in enumerate(y_peers):
        remote(pooled.at[mine], pooled.at[mine], v_send.at[i], v_recv.at[y], p, vocab)
    for o in range(1, 4):
        yy = (y + o) % 4
        pltpu.make_async_copy(pooled.at[xc * 4 + yy], pooled.at[xc * 4 + yy], v_recv.at[yy]).wait()
    line = pl.ds(xc * 4, 4)
    for i, p in enumerate(xc_dp):
        remote(pooled.at[line], pooled.at[line], g_send.at[i], g_recv.at[xc], p, vocab)
    for p in xc_peers:
        block = pooled.at[pl.ds(p * 4, 4)]
        pltpu.make_async_copy(block, block, g_recv.at[p]).wait()

    flat = pooled[...].reshape(512, 256)
    for i in range(4):
        both[:, pl.ds(256 * i, 256)] = jnp.dot(select[i], flat, preferred_element_type=F32).astype(BF)
    passages = both[pl.ds(0, PAIRS), :]
    twice[pl.ds(0, PAIRS), :] = passages
    twice[pl.ds(PAIRS, PAIRS), :] = passages
    nt = (((1,), (1,)), ((), ()))
    part_scores[...] = lax.dot_general(both[pl.ds(PAIRS, PAIRS), :], twice[...], nt, preferred_element_type=F32)

    rows8 = pl.ds(pl.multiple_of(xc * 8, 8), 8)
    low_lanes = lax.broadcasted_iota(jnp.int32, (16, 128), 1) < PAIRS
    first_rows = pl.ds(pl.multiple_of(core * 32, 16), 16)
    next_rows = pl.ds(pl.multiple_of(core * 32 + 16, 16), 16)
    score_parts[vocab] = jnp.where(low_lanes, part_scores[first_rows, :], part_scores[next_rows, :])
    all_known()
    for i, p in enumerate(vocab_peers):
        remote(score_parts.at[vocab], score_parts.at[vocab], s_send.at[i], s_recv.at[vocab], dp, p)
    for p in vocab_peers:
        pltpu.make_async_copy(score_parts.at[p], score_parts.at[p], s_recv.at[p]).wait()
    summed_parts = jnp.sum(score_parts[...], axis=0)
    scores = SCORE_SCALE * jnp.concatenate([summed_parts, pltpu.roll(summed_parts, PAIRS, 1)], axis=0)
    valid = lax.broadcasted_iota(jnp.int32, (32, 128), 1) < PAIRS
    top = jnp.max(jnp.where(valid, scores, -jnp.inf), axis=1, keepdims=True)
    shifted = jnp.where(valid, jnp.exp(jnp.where(valid, scores - top, 0.0)), 0.0)
    soft = shifted / jnp.sum(shifted, axis=1, keepdims=True)
    grads[pl.ds(core, 1)] = (LOSS_SCALE * (soft - row_targets[...].reshape(32, 128))).reshape(1, 32, 128)
    remote(grads.at[core], grads.at[core], d_send.at[0], d_recv.at[core], sibling, vocab)
    pltpu.make_async_copy(grads.at[1 - core], grads.at[1 - core], d_recv.at[1 - core]).wait()
    whole = jnp.concatenate([grads[...].reshape(PAIRS, 128), jnp.zeros((PAIRS, 128), F32)], axis=0)
    grads_t[...] = whole.T

    def exact_dot(lhs, rhs):
        a = lhs.astype(BF)
        rest = lhs - a.astype(F32)
        b = rest.astype(BF)
        c = (rest - b.astype(F32)).astype(BF)
        out = jnp.dot(c, rhs, preferred_element_type=F32)
        out = out + jnp.dot(b, rhs, preferred_element_type=F32)
        return out + jnp.dot(a, rhs, preferred_element_type=F32)

    rows8_here = pl.ds(pl.multiple_of(x * 8, 8), 8)
    q_grad = exact_dot(grads[core, rows8_here, :][:, :PAIRS], both[pl.ds(0, PAIRS), :])
    p_grad = exact_dot(grads_t[rows8, :][:, :PAIRS], both[pl.ds(PAIRS, PAIRS), :])
    srow = lax.broadcasted_iota(jnp.int32, (8, SLICE), 0)
    for n, (start, size) in enumerate(SEGMENTS):
        grad = q_grad if n < 2 else p_grad
        one = jnp.sum(jnp.where(srow == 2 * y + n % 2, grad, 0.0), axis=0, keepdims=True)
        vecs[pl.ds(n, 1), :] = (SCORE_SCALE * one) / sums[pl.ds(n, 1), :]

    def finish(b, carry):
        cols = pl.ds(pl.multiple_of(b * 128, 128), 128)
        for n, (start, size) in enumerate(SEGMENTS):
            lgrad[pl.ds(start, size), cols] = (act[pl.ds(start, size), cols] * vecs[pl.ds(n, 1), cols]).astype(BF)
        return carry

    lax.fori_loop(0, 8, finish, 0)
    lgrad[...] = jnp.dot(spread[...], lgrad[...], preferred_element_type=F32).astype(BF)

    up, down = ((z + 1) % 8) * 2 + hi, ((z + 7) % 8) * 2 + hi
    across = z * 2 + 1 - hi

    def cols_of(c):
        return pl.ds(c * COLS, COLS)

    def own_part(c, k):
        place = (z + k + 8) % 8
        if c < EARLY:
            return summed[c, place]
        return part[pl.ds(pl.multiple_of(place * CHUNK, CHUNK), CHUNK), cols_of(c)]

    def hop(c, i, value, to):
        if c < EARLY:
            out_slot, in_slot = near_out.at[c, i], near_in.at[c, i]
        else:
            out_slot, in_slot = chain_out.at[c - EARLY, i], chain_in.at[c - EARLY, i]
        out_slot[...] = value.astype(BF)
        remote(out_slot, in_slot, c_send.at[c, i], c_recv.at[c, i], dp, to)

    def landed(c, i):
        in_slot = near_in.at[c, i] if c < EARLY else chain_in.at[c - EARLY, i]
        pltpu.make_async_copy(in_slot, in_slot, c_recv.at[c, i]).wait()
        return in_slot[...].astype(F32)

    def chain(c, s):
        a = 4 if c % 2 == 0 else 3
        b = 7 - a
        if s == 0:
            hop(c, 0, own_part(c, a), up)
            hop(c, a, own_part(c, -b), down)
        elif s < 4:
            if s < a:
                hop(c, s, landed(c, s - 1) + own_part(c, a - s), up)
            if s < b:
                hop(c, a + s, landed(c, a + s - 1) + own_part(c, s - b), down)
        else:
            return own_part(c, 0) + landed(c, a - 1) + landed(c, 6)

    def product(c):
        part[:, cols_of(c)] = lax.dot_general(lgrad[...], wf[cols_of(c), :], nt, preferred_element_type=F32)

    def group(c, place, h):
        return part[pl.ds(pl.multiple_of(place * CHUNK + h * GROUP, GROUP), GROUP), cols_of(c)]

    def early(c, s):
        if s == 0:
            product(c)
            for place in range(8):
                wide_out[c, place] = group(c, place, 1 - hi).astype(BF)
            remote(wide_out.at[c], wide_in.at[c], y_send.at[c], y_recv.at[c], dp, across)
        elif s == 1:
            pltpu.make_async_copy(wide_in.at[c], wide_in.at[c], y_recv.at[c]).wait()
            for place in range(8):
                summed[c, place] = group(c, place, hi) + wide_in[c, place].astype(F32)
            chain(c, 0)
        elif s < 5:
            chain(c, s - 1)
        else:
            out_ref[:, cols_of(c)] = chain(c, 4)[:OWN].astype(BF)

    def late(c, s):
        if s == 0:
            product(c)
        if s < 4:
            chain(c, s)
        elif s == 4:
            kept[c] = chain(c, 4)
            swap_out[c] = kept[c, pl.ds(pl.multiple_of((1 - hi) * GROUP, GROUP), GROUP), :].astype(BF)
            remote(swap_out.at[c], swap_in.at[c], y_send.at[c], y_recv.at[c], dp, across)
        else:
            pltpu.make_async_copy(swap_in.at[c], swap_in.at[c], y_recv.at[c]).wait()
            total = kept[c, pl.ds(pl.multiple_of(hi * GROUP, GROUP), GROUP), :] + swap_in[c].astype(F32)
            out_ref[:, cols_of(c)] = total[:OWN].astype(BF)

    def when(c, s):
        if c < EARLY:
            return (STREAMS * s + c + (LAG if s else 0), c)
        return (STREAMS * s + c, c)

    for c, s in sorted(((c, s) for c in range(STREAMS) for s in range(6)), key=lambda e: when(*e)):
        (early if c < EARLY else late)(c, s)

    for cond, copy in sends:
        if cond is None:
            copy.wait_send()
        else:
            pl.when(cond)(copy.wait_send)
    for copy in copies:
        copy.wait_send()


def per_device(hidden, head_weight, head_bias, lengths, positives):
    vmem, smem = pltpu.VMEM, pltpu.SMEM
    dma = pltpu.SemaphoreType.DMA
    return pl.pallas_call(
        kernel,
        out_shape=jax.ShapeDtypeStruct((OWN, WIDTH), BF),
        in_specs=[
            pl.BlockSpec(memory_space=pl.ANY),
            pl.BlockSpec(memory_space=pl.ANY),
            pl.BlockSpec(memory_space=pl.ANY),
            pl.BlockSpec(memory_space=pl.ANY),
            pl.BlockSpec(memory_space=pl.ANY),
        ],
        out_specs=pl.BlockSpec(memory_space=vmem),
        scratch_shapes=[
            vmem((1, SLICE), F32),
            smem((2, 2), jnp.int32),
            smem((2,), jnp.int32),
            vmem((ROWS, WIDTH), BF),
            vmem((WIDTH, SLICE), BF),
            vmem((ROWS, SLICE), F32),
            vmem((8, SLICE), F32),
            vmem((8, SLICE), F32),
            vmem((16, 256), F32),
            vmem((32, 16, 256), BF),
            vmem((4, 128, 512), BF),
            vmem((256, 256), BF),
            vmem((128, SLICE), BF),
            vmem((128, SLICE), BF),
            vmem((PAIRS, 128), F32),
            vmem((16, 16, 128), F32),
            vmem((2, 32, 128), F32),
            vmem((128, 128), F32),
            vmem((4, 8, 128), F32),
            vmem((4, 8, 128), F32),
            vmem((256, SLICE), BF),
            vmem((256, WIDTH), F32),
            vmem((STREAMS - EARLY, 7, CHUNK, COLS), BF),
            vmem((STREAMS - EARLY, 7, CHUNK, COLS), BF),
            vmem((STREAMS, CHUNK, COLS), F32),
            vmem((STREAMS, GROUP, COLS), BF),
            vmem((STREAMS, GROUP, COLS), BF),
            vmem((EARLY, 8, GROUP, COLS), BF),
            vmem((EARLY, 8, GROUP, COLS), BF),
            vmem((EARLY, 7, GROUP, COLS), BF),
            vmem((EARLY, 7, GROUP, COLS), BF),
            vmem((EARLY, 8, GROUP, COLS), F32),
            dma((5,)),
            dma((128,)), dma((96,)),
            dma((3,)), dma((4,)),
            dma((3,)), dma((4,)),
            dma((3,)), dma((4,)),
            dma((7,)), dma((8,)),
            dma((15,)), dma((16,)),
            dma((1,)), dma((2,)),
            dma((STREAMS, 7)), dma((STREAMS, 7)),
            dma((STREAMS,)), dma((STREAMS,)),
            pltpu.SemaphoreType.REGULAR, pltpu.SemaphoreType.REGULAR, pltpu.SemaphoreType.REGULAR,
        ],
        compiler_params=pltpu.CompilerParams(
            collective_id=0, has_side_effects=True, vmem_limit_bytes=63 * 1024 * 1024
        ),
        cost_estimate=pl.CostEstimate(flops=4 * ROWS * WIDTH * SLICE, bytes_accessed=4 * 1024 * 1024, transcendentals=3 * ROWS * SLICE),
    )(hidden, head_weight, head_bias.reshape(1, SLICE), lengths, positives)


def solution(mesh):
    return jax.shard_map(
        per_device,
        mesh=mesh,
        in_specs=(P("dp", None), P("dp", "vocab"), P("vocab"), P("dp", None), P("dp")),
        out_specs=P(("dp", "vocab"), None),
        check_vma=False,
    )
```
